32 devices in a mesh: section: 4 (over x, core), fsdp: 2 (over y), ep: 4 (over z).
Axes of the slice: x: 2, y: 2, z: 4, core: 2. Of those that a mesh axis runs over, the one named last changes fastest.
Arguments:
- hidden: bfloat16 [2048, 7168], P(('section', 'fsdp'), 'ep'), may hold values from -6 to 6
- attn_gain: float32 [7168], replicated, may hold values from 0.25 to 1.75
- q_gain: float32 [1536], replicated, may hold values from 0.25 to 1.75
- kv_gain: float32 [512], replicated, may hold values from 0.25 to 1.75
- down_weight: bfloat16 [7168, 2112], P('fsdp', 'ep'), may hold values from -0.0625 to 0.0625
Outputs:
- q_latent: bfloat16 [2048, 1536], P(('section', 'fsdp', 'ep'))
- kv_cache: bfloat16 [2048, 576], P(('section', 'fsdp', 'ep'))
The draws below stay inside these ranges and needn't reach their ends.
All inputs are finite; a program needn't handle non-finite values.
Results may differ from the reference program's by a relative error of at most 0.0049.
Values may be sent and summed in bfloat16 or wider, within the bound.
No kernel may reach another device: no remote copies, remote signals or barrier semaphores. Data moves between devices by JAX's collectives and lax.ppermute only.
A program may use at most 64 MiB of HBM per device.

```python
import jax
import jax.numpy as jnp
from jax import lax

D = 7168
QL = 1536
KVL = 512
ROPE = 64
TOK_DEV = 256
LENGTH = 4096
LAT = 2112
TOKENS = 2048
N_FSDP = 2


def block_levels(own_key, dims, split, low, largest):
    level, own = 1.0, jax.random.fold_in(own_key, 6)
    for dim, parts in split:
        heights = jnp.exp(jax.random.uniform(jax.random.fold_in(own, dim), (parts,), jnp.float32, low / len(split), largest / len(split)))
        level = level * jnp.repeat(heights, dims[dim] // parts).reshape([-1 if axis == dim else 1 for axis in range(len(dims))])
    return level


def bell_draw(own_key, shape, scale, reach, cuts=(), held_as=jnp.bfloat16):
    level = block_levels(own_key, shape, cuts, -0.22, 0.18) if cuts else 1.0
    values = jax.random.normal(own_key, shape, jnp.float32) * scale * level
    return jnp.minimum(jnp.maximum(values, -reach), reach).astype(held_as)


def setup_inputs(seed: int = 0) -> dict:
    splits = jax.random.split(jax.random.key(seed), 6)
    hidden = bell_draw(splits[0], (TOKENS, D), 1.0, 6.0, ((0, 8), (1, 4)))
    attn_gain = jnp.clip(1.0 + 0.15 * jax.random.normal(splits[1], (D,), jnp.float32), 0.25, 1.75)
    q_gain = jnp.clip(1.0 + 0.15 * jax.random.normal(splits[2], (QL,), jnp.float32), 0.25, 1.75)
    kv_gain = jnp.clip(1.0 + 0.15 * jax.random.normal(splits[3], (KVL,), jnp.float32), 0.25, 1.75)
    down_weight = bell_draw(splits[4], (D, LAT), D ** -0.5, 0.0625, ((0, 2), (1, 4)))
    return {"hidden": hidden, "attn_gain": attn_gain, "q_gain": q_gain, "kv_gain": kv_gain, "down_weight": down_weight}


epsilon = 1e-06
rope_base = 10000.0

def root_scale(values, gain):
    mean_square = lax.optimization_barrier(jnp.mean(values * values, axis=-1, keepdims=True))
    return values * lax.rsqrt(mean_square + epsilon) * gain

def rotate(latent, position):
    half_rope = ROPE // 2
    frequency = rope_base ** (-(jnp.arange(half_rope).astype(jnp.float32) / half_rope))
    angle = position.astype(jnp.float32)[:, None] * frequency[None, :]
    first = latent[:, QL + KVL:QL + KVL + half_rope]
    second = latent[:, QL + KVL + half_rope:]
    cosine = jnp.cos(angle)
    sine = jnp.sin(angle)
    return jnp.concatenate([first * cosine - second * sine, second * cosine + first * sine], axis=1)

def reference(hidden, attn_gain, q_gain, kv_gain, down_weight):
    section_rows = TOK_DEV * N_FSDP
    moved = jnp.roll(hidden, section_rows, axis=0)
    grouped = moved.reshape(TOKENS // TOK_DEV, TOK_DEV, D)

    def one_block(index_rows):
        index, rows = index_rows
        normed = root_scale(rows.astype(jnp.float32), attn_gain).astype(jnp.bfloat16)
        latent = jnp.dot(normed, down_weight, preferred_element_type=jnp.float32)
        query = root_scale(latent[:, :QL], q_gain).astype(jnp.bfloat16)
        key_value = root_scale(latent[:, QL:QL + KVL], kv_gain)
        row_index = index * TOK_DEV + jnp.arange(TOK_DEV).astype(jnp.int32)
        position = row_index % section_rows % LENGTH
        cache = jnp.concatenate([key_value, rotate(latent, position)], axis=1).astype(jnp.bfloat16)
        return (query, cache)
    indices = jnp.arange(TOKENS // TOK_DEV).astype(jnp.int32)
    query, cache = lax.map(one_block, (indices, grouped))
    return (query.reshape(TOKENS, QL), cache.reshape(TOKENS, KVL + ROPE))
```

```python
import jax
import jax.numpy as jnp
from jax import lax
from jax.sharding import PartitionSpec as P

QL = 1536
KVL = 512
ROPE = 64
LENGTH = 4096


epsilon = 1e-06
rope_base = 10000.0
ROW_CHUNKS = 2
WEIGHT_CHUNKS = 2


def root_scale(values, gain):
    mean_square = jnp.mean(values * values, axis=-1, keepdims=True)
    return values * lax.rsqrt(mean_square + epsilon) * gain


def rotate(latent, position):
    half_rope = ROPE // 2
    frequency = rope_base ** (-(jnp.arange(half_rope).astype(jnp.float32) / half_rope))
    angle = position.astype(jnp.float32)[:, None] * frequency[None, :]
    first = latent[:, QL + KVL : QL + KVL + half_rope]
    second = latent[:, QL + KVL + half_rope :]
    cosine = jnp.cos(angle)
    sine = jnp.sin(angle)
    return jnp.concatenate([first * cosine - second * sine, second * cosine + first * sine], axis=1)


def whole_weight(weight):
    fsdp, section = lax.axis_size("fsdp"), lax.axis_size("section")
    columns, depth = weight.shape
    if fsdp != 2 or section != 4:
        return lax.all_gather(weight, "fsdp", axis=1, tiled=True)
    section_index, fsdp_index = lax.axis_index("section"), lax.axis_index("fsdp")
    quarter = depth // section
    part = quarter // WEIGHT_CHUNKS
    other = (1 - fsdp_index) * depth
    full = jnp.zeros((columns, fsdp * depth), weight.dtype)
    full = lax.dynamic_update_slice(full, weight, (0, fsdp_index * depth))
    for chunk in range(WEIGHT_CHUNKS):
        own = lax.dynamic_slice(weight, (0, section_index * quarter + chunk * part), (columns, part))
        here = lax.ppermute(own, "fsdp", [(0, 1), (1, 0)])
        across = lax.ppermute(here, "section", [(i, i ^ 2) for i in range(4)])
        beside = lax.ppermute(here, "section", [(i, i ^ 1) for i in range(4)])
        beside_across = lax.ppermute(across, "section", [(i, i ^ 1) for i in range(4)])
        for flip, piece in ((0, here), (1, beside), (2, across), (3, beside_across)):
            start = other + (section_index ^ flip) * quarter + chunk * part
            full = lax.dynamic_update_slice(full, piece, (0, start))
    return full


def on_device(hidden, attn_gain, q_gain, kv_gain, down_weight):
    row_count, width = hidden.shape
    ep, section = lax.axis_size("ep"), lax.axis_size("section")
    ep_index = lax.axis_index("ep")
    rows = row_count // ROW_CHUNKS
    own = [hidden[i * rows : (i + 1) * rows] for i in range(ROW_CHUNKS)]
    up = [(i, i + 1) for i in range(ep - 1)]
    down = [(i + 1, i) for i in range(ep - 1)]
    arrivals = [[(block, 0)] for block in own]
    rising, falling = list(own), list(own)
    for step in range(1, ep):
        for i in range(ROW_CHUNKS):
            rising[i] = lax.ppermute(rising[i], "ep", up)
            falling[i] = lax.ppermute(falling[i], "ep", down)
            arrivals[i] += [(rising[i], -step), (falling[i], step)]
    weight = whole_weight(down_weight.T)
    latents = []
    for i in range(ROW_CHUNKS):
        total, squares = 0.0, 0.0
        for block, offset in arrivals[i]:
            place = jnp.clip(ep_index + offset, 0, ep - 1) * width
            values = block.astype(jnp.float32)
            squares = squares + jnp.sum(values * values, axis=1, keepdims=True)
            gained = (values * lax.dynamic_slice(attn_gain, (place,), (width,))).astype(jnp.bfloat16)
            total = total + lax.dot_general(
                gained,
                lax.dynamic_slice(weight, (0, place), (weight.shape[0], width)),
                (((1,), (1,)), ((), ())),
                preferred_element_type=jnp.float32,
            )
        scale = lax.rsqrt(squares / (ep * width) + epsilon)
        latents.append((total * scale).astype(jnp.bfloat16))
    mine = jnp.concatenate(latents, axis=0)
    quarter = row_count // ep
    columns = mine.shape[1]
    latent = jnp.zeros((ep, quarter, columns), jnp.bfloat16)
    for turn in range(ep):
        target = (ep_index + turn) % ep
        piece = lax.dynamic_slice(mine, (target * quarter, 0), (quarter, columns))
        moves = [
            (s * ep + e, (s + 1) % section * ep + (e + turn) % ep)
            for s in range(section)
            for e in range(ep)
        ]
        piece = lax.ppermute(piece, ("section", "ep"), moves)
        source = (ep_index + ep - turn) % ep
        latent = lax.dynamic_update_slice(latent, piece[None], (source, 0, 0))
    latent = latent.astype(jnp.float32).transpose(1, 0, 2).reshape(quarter, ep * columns)
    query = root_scale(latent[:, :QL], q_gain).astype(jnp.bfloat16)
    key_value = root_scale(latent[:, QL : QL + KVL], kv_gain)
    row_index = lax.axis_index("fsdp") * row_count + ep_index * quarter + jnp.arange(quarter)
    position = row_index % LENGTH
    cache = jnp.concatenate([key_value, rotate(latent, position)], axis=1).astype(jnp.bfloat16)
    return (query, cache)


def solution(mesh):
    placed = (P(("section", "fsdp"), "ep"), P(), P(), P(), P("fsdp", "ep"))
    return jax.shard_map(
        on_device,
        mesh=mesh,
        in_specs=placed,
        out_specs=(P(("section", "fsdp", "ep"), None), P(("section", "fsdp", "ep"), None)),
        check_vma=False,
    )
```

```python
import functools

import jax
import jax.numpy as jnp
from jax import lax
from jax.experimental import pallas as pl
from jax.experimental.pallas import tpu as pltpu
from jax.sharding import PartitionSpec as P

QL = 1536
KVL = 512
ROPE = 64
LENGTH = 4096


epsilon = 1e-06
rope_base = 10000.0
ROW_CHUNKS = 1
PACK = 16


def root_scale(values, gain):
    mean_square = jnp.mean(values * values, axis=-1, keepdims=True)
    return values * lax.rsqrt(mean_square + epsilon) * gain


def rotate(latent, position):
    half_rope = ROPE // 2
    frequency = rope_base ** (-(jnp.arange(half_rope).astype(jnp.float32) / half_rope))
    angle = position.astype(jnp.float32)[:, None] * frequency[None, :]
    first = latent[:, QL + KVL : QL + KVL + half_rope]
    second = latent[:, QL + KVL + half_rope :]
    cosine = jnp.cos(angle)
    sine = jnp.sin(angle)
    return jnp.concatenate([first * cosine - second * sine, second * cosine + first * sine], axis=1)


def weight_parts(weight, width):
    fsdp, section = lax.axis_size("fsdp"), lax.axis_size("section")
    columns, depth = weight.shape
    if fsdp != 2 or section != 4 or depth != 2 * width:
        full = lax.all_gather(weight, "fsdp", axis=1, tiled=True)
        return [[full]], lambda block: (0 * block, block)
    side, fsdp_index = lax.axis_index("section") % 2, lax.axis_index("fsdp")
    cut = (columns // 2 + PACK - 1) // PACK * PACK
    here, beside = [], []
    for low, high in ((0, cut), (cut, columns)):
        own = lax.dynamic_slice(weight, (low, side * width), (high - low, width))
        here.append(lax.ppermute(own, "fsdp", [(0, 1), (1, 0)]))
        beside.append(lax.ppermute(here[-1], "section", [(i, i ^ 1) for i in range(4)]))

    def place(block):
        local = block // 2 == fsdp_index
        return jnp.where(local, 0, jnp.where(block % 2 == side, 1, 2)), jnp.where(local, block % 2, 0)

    return [[weight], here, beside], place


def accumulate(layout, blocks, first, last, width, where, *refs):
    refs = list(refs)
    block_refs = [refs.pop(0) for _ in range(blocks)]
    part_refs = [[refs.pop(0) for _ in range(count)] for count in layout]
    gain_ref = refs.pop(0)
    if not first:
        total_in, squares_in = refs.pop(0), refs.pop(0)
    total_out, squares_out = refs.pop(0), refs.pop(0)
    weights, arrived = refs
    if first:
        total_out[...] = jnp.zeros_like(total_out)
        squares_out[...] = jnp.zeros_like(squares_out)
    else:
        total_out[...] = total_in[...]
        squares_out[...] = squares_in[...]

    def fetch(index, part):
        copies, row = [], 0
        for ref in part_refs[part]:
            rows = ref.shape[0]
            start = pl.multiple_of(where[3, index] * width, width)
            copies.append(
                pltpu.make_async_copy(
                    ref.at[:, pl.ds(start, width)],
                    weights.at[index, pl.ds(row, rows)],
                    arrived.at[index, len(copies)],
                )
            )
            row += rows
        return copies

    for index in range(blocks):
        for part in range(len(part_refs)):

            @pl.when((where[0, index] == 1) & (where[2, index] == part))
            def _():
                for copy in fetch(index, part):
                    copy.start()

    for index in range(blocks):

        @pl.when(where[0, index] == 1)
        def _():
            values = block_refs[index][...].astype(jnp.float32)
            squares_out[...] += jnp.sum(values * values, axis=1, keepdims=True)
            start = pl.multiple_of(where[1, index] * width, width)
            gained = (values * gain_ref[:, pl.ds(start, width)]).astype(jnp.bfloat16)
            for part in range(len(part_refs)):

                @pl.when(where[2, index] == part)
                def _():
                    for copy in fetch(index, part):
                        copy.wait()

            total_out[...] += lax.dot_general(
                gained,
                weights[index],
                (((1,), (1,)), ((), ())),
                preferred_element_type=jnp.float32,
            )


def multiply(blocks, where, parts, gain, carried):
    rows, width = blocks[0].shape
    columns = sum(array.shape[0] for array in parts[0])
    layout = tuple(len(part) for part in parts)
    vmem, anywhere = pl.BlockSpec(memory_space=pltpu.VMEM), pl.BlockSpec(memory_space=pl.ANY)
    flat = [array for part in parts for array in part]
    return pl.pallas_call(
        functools.partial(accumulate, layout, len(blocks), carried is None, False, width),
        out_shape=(
            jax.ShapeDtypeStruct((rows, columns), jnp.float32),
            jax.ShapeDtypeStruct((rows, 1), jnp.float32),
        ),
        in_specs=[pl.BlockSpec(memory_space=pltpu.SMEM)]
        + [vmem] * len(blocks)
        + [anywhere] * len(flat)
        + [vmem]
        + [vmem] * (0 if carried is None else 2),
        out_specs=(vmem, vmem),
        scratch_shapes=[
            pltpu.VMEM((len(blocks), columns, width), jnp.bfloat16),
            pltpu.SemaphoreType.DMA((len(blocks), max(layout))),
        ],
        compiler_params=pltpu.CompilerParams(vmem_limit_bytes=32 * 1024 * 1024),
        cost_estimate=pl.CostEstimate(
            flops=2 * rows * width * columns * len(blocks),
            bytes_accessed=2 * width * (rows + columns) * len(blocks),
            transcendentals=0,
        ),
    )(where, *blocks, *flat, gain, *(carried or ()))


def on_device(hidden, attn_gain, q_gain, kv_gain, down_weight):
    row_count, width = hidden.shape
    ep, section = lax.axis_size("ep"), lax.axis_size("section")
    ep_index = lax.axis_index("ep")
    up = [(i, i + 1) for i in range(ep - 1)]
    down = [(i + 1, i) for i in range(ep - 1)]
    rising, falling = [hidden], [hidden]
    for step in range(1, ep):
        rising.append(lax.ppermute(rising[-1], "ep", up))
        falling.append(lax.ppermute(falling[-1], "ep", down))
    parts, place = weight_parts(down_weight.T, width)
    gain = attn_gain.reshape(1, -1)

    def add(pairs, carried):
        wheres = []
        for _, offset in pairs:
            block = ep_index + offset
            valid = (block >= 0) & (block < ep)
            block = jnp.clip(block, 0, ep - 1)
            part, inside = place(block)
            wheres.append(jnp.stack([valid.astype(jnp.int32), block, part, inside]))
        where = jnp.stack(wheres, axis=1).astype(jnp.int32)
        return multiply([block for block, _ in pairs], where, parts, gain, carried)

    near = [(hidden, 0)]
    for step in range(1, ep - 1):
        near += [(rising[step], -step), (falling[step], step)]
    total, squares = add(near, None)
    total, squares = add([(rising[-1], 1 - ep), (falling[-1], ep - 1)], (total, squares))
    mine = (total * lax.rsqrt(squares / (ep * width) + epsilon)).astype(jnp.bfloat16)
    quarter = row_count // ep
    columns = mine.shape[1]
    latent = jnp.zeros((ep, quarter, columns), jnp.bfloat16)
    for turn in range(ep):
        target = (ep_index + turn) % ep
        piece = lax.dynamic_slice(mine, (target * quarter, 0), (quarter, columns))
        moves = [
            (s * ep + e, (s + 1) % section * ep + (e + turn) % ep)
            for s in range(section)
            for e in range(ep)
        ]
        piece = lax.ppermute(piece, ("section", "ep"), moves)
        source = (ep_index + ep - turn) % ep
        latent = lax.dynamic_update_slice(latent, piece[None], (source, 0, 0))
    latent = latent.astype(jnp.float32).transpose(1, 0, 2).reshape(quarter, ep * columns)
    query = root_scale(latent[:, :QL], q_gain).astype(jnp.bfloat16)
    key_value = root_scale(latent[:, QL : QL + KVL], kv_gain)
    row_index = lax.axis_index("fsdp") * row_count + ep_index * quarter + jnp.arange(quarter)
    position = row_index % LENGTH
    cache = jnp.concatenate([key_value, rotate(latent, position)], axis=1).astype(jnp.bfloat16)
    return (query, cache)


def solution(mesh):
    placed = (P(("section", "fsdp"), "ep"), P(), P(), P(), P("fsdp", "ep"))
    return jax.shard_map(
        on_device,
        mesh=mesh,
        in_specs=placed,
        out_specs=(P(("section", "fsdp", "ep"), None), P(("section", "fsdp", "ep"), None)),
        check_vma=False,
    )
```

```python
import functools

import jax
import jax.numpy as jnp
from jax import lax
from jax.experimental import pallas as pl
from jax.experimental.pallas import tpu as pltpu
from jax.sharding import PartitionSpec as P

QL = 1536
KVL = 512
ROPE = 64
LENGTH = 4096


epsilon = 1e-06
rope_base = 10000.0
ROW_CHUNKS = 2
PACK = 16
LANES = 128
VMEM_LIMIT = 48 * 1024 * 1024

vmem = pl.BlockSpec(memory_space=pltpu.VMEM)
smem = pl.BlockSpec(memory_space=pltpu.SMEM)
anywhere = pl.BlockSpec(memory_space=pl.ANY)


def section_spread(piece, pairs_of):
    across = lax.ppermute(piece, *pairs_of(2))
    beside = lax.ppermute(piece, *pairs_of(1))
    beside_across = lax.ppermute(across, *pairs_of(1))
    return [piece, beside, across, beside_across]


def far_weight(weight, width):
    columns = weight.shape[0]
    section_index, fsdp_index = lax.axis_index("section"), lax.axis_index("fsdp")
    low = section_index * LANES
    own = lax.dynamic_slice(weight, (low, fsdp_index * width), (columns - 3 * LANES, width))
    own = lax.ppermute(own, ("fsdp", "ep"), [(4, 5), (3, 2)])
    other = lax.ppermute(own, ("fsdp", "ep"), [(5, 1), (2, 6)])
    home = (lax.axis_index("ep") == 1) == (fsdp_index == 1)
    piece = jnp.where(home, own, other)

    def pairs_of(flip):
        return ("section", "ep"), [(s * 4 + z, (s ^ flip) * 4 + z) for s in range(4) for z in (1, 2)]

    return section_spread(piece, pairs_of)


def other_weight(weight, width):
    columns, depth = weight.shape
    section_index = lax.axis_index("section")
    quarter = depth // 4
    cut = (columns // 2 + PACK - 1) // PACK * PACK
    pieces = []
    for low, high in ((0, cut), (cut, columns)):
        own = lax.dynamic_slice(weight, (low, section_index * quarter), (high - low, quarter))
        own = lax.ppermute(own, "fsdp", [(0, 1), (1, 0)])
        pieces.append(
            section_spread(own, lambda flip: ("section", [(s, s ^ flip) for s in range(4)]))
        )
    return [[pieces[cut][flip] for cut in range(2)] for flip in range(4)]


def weight_copies(where, index, local_ref, piece_refs, target, arrived, act):
    width = target.shape[1]

    @pl.when(where[2, index] == 1)
    def _():
        start = pl.multiple_of(where[3, index] * width, width)
        act(pltpu.make_async_copy(local_ref.at[:, pl.ds(start, width)], target, arrived.at[0]))

    if piece_refs:
        for half in range(2):
            for flip in range(4):

                @pl.when((where[2, index] == 0) & (where[4 + half, index] == flip))
                def _():
                    row = 0
                    for cut, ref in enumerate(piece_refs[flip]):
                        rows, columns = ref.shape
                        into = target.at[pl.ds(row, rows), pl.ds(half * columns, columns)]
                        act(pltpu.make_async_copy(ref, into, arrived.at[2 * half + cut]))
                        row += rows


def start(copy):
    copy.start()


def wait(copy):
    copy.wait()


def product(values, gain, weight):
    gained = (values * gain).astype(jnp.bfloat16)
    return lax.dot_general(
        gained, weight, (((1,), (1,)), ((), ())), preferred_element_type=jnp.float32
    )


def near_kernel(groups, chunks, pieces, where, *refs):
    refs = list(refs)
    block_refs = [[refs.pop(0) for _ in range(chunks)] for _ in range(groups)]
    gain_ref, local_ref = refs.pop(0), refs.pop(0)
    piece_refs = [[refs.pop(0) for _ in range(2)] for _ in range(pieces)]
    total_ref, squares_ref, blocks, weights, block_arrived, weight_arrived = refs
    rows, width = block_refs[0][0].shape

    def block_copies(index, act):
        for chunk, ref in enumerate(block_refs[index]):
            into = blocks.at[index, pl.ds(chunk * rows, rows)]
            act(pltpu.make_async_copy(ref, into, block_arrived.at[index, chunk]))

    for index in range(groups):

        @pl.when(where[0, index] == 1)
        def _():
            block_copies(index, start)
            weight_copies(
                where, index, local_ref, piece_refs, weights.at[index], weight_arrived.at[index], start
            )

    total_ref[...] = jnp.zeros_like(total_ref)
    squares_ref[...] = jnp.zeros_like(squares_ref)
    for index in range(groups):

        @pl.when(where[0, index] == 1)
        def _():
            block_copies(index, wait)
            weight_copies(
                where, index, local_ref, piece_refs, weights.at[index], weight_arrived.at[index], wait
            )
            values = blocks[index].astype(jnp.float32)
            squares_ref[...] += jnp.sum(values * values, axis=1, keepdims=True)
            at = pl.multiple_of(where[1, index] * width, width)
            total_ref[...] += product(values, gain_ref[:, pl.ds(at, width)], weights[index])


def far_kernel(chunks, pieces, far_pieces, where, *refs):
    refs = list(refs)
    block_refs = [[refs.pop(0) for _ in range(chunks)] for _ in range(2)]
    gain_ref, total_in, squares_in, local_ref = [refs.pop(0) for _ in range(4)]
    piece_refs = [[refs.pop(0) for _ in range(2)] for _ in range(pieces)]
    far_refs = [refs.pop(0) for _ in range(far_pieces)]
    out_refs = [refs.pop(0) for _ in range(4)]
    total, extra, squares, block, weight, far, block_arrived, weight_arrived, far_arrived = refs
    rows, width = block_refs[0][0].shape

    def block_copies(act):
        for side in range(2):

            @pl.when(where[0, 0] == side)
            def _():
                for chunk, ref in enumerate(block_refs[side]):
                    into = block.at[pl.ds(chunk * rows, rows)]
                    act(pltpu.make_async_copy(ref, into, block_arrived.at[chunk]))

    def far_copies(act):
        if far_pieces == 1:
            act(pltpu.make_async_copy(far_refs[0], far, far_arrived.at[0]))
            return
        for flip in range(far_pieces):
            for place in range(4):
                count = LANES if place < 3 else far.shape[0] - 3 * LANES

                @pl.when(where[7, 0] == flip ^ place)
                def _():
                    act(
                        pltpu.make_async_copy(
                            far_refs[flip].at[pl.ds(0, count)],
                            far.at[pl.ds(place * LANES, count)],
                            far_arrived.at[flip],
                        )
                    )

    inner = where[6, 0] == 1
    block_copies(start)
    weight_copies(where, 0, local_ref, piece_refs, weight, weight_arrived, start)

    @pl.when(inner)
    def _():
        far_copies(start)

    block_copies(wait)
    values = block[...].astype(jnp.float32)
    squares[...] = squares_in[...] + jnp.sum(values * values, axis=1, keepdims=True)
    at = pl.multiple_of(where[1, 0] * width, width)
    gained = (values * gain_ref[:, pl.ds(at, width)]).astype(jnp.bfloat16)
    contract = (((1,), (1,)), ((), ()))
    weight_copies(where, 0, local_ref, piece_refs, weight, weight_arrived, wait)
    total[...] = total_in[...] + lax.dot_general(
        gained, weight[...], contract, preferred_element_type=jnp.float32
    )
    extra[...] = jnp.zeros_like(extra)

    @pl.when(inner)
    def _():
        far_copies(wait)
        extra[...] = lax.dot_general(
            gained, far[...], contract, preferred_element_type=jnp.float32
        )

    quarter, columns = out_refs[0].shape[0], total.shape[1]
    main = columns // LANES * LANES
    for turn, out_ref in enumerate(out_refs):
        piece = pl.ds(pl.multiple_of(where[8, turn] * quarter, quarter), quarter)
        own, more, square = total[piece, :], extra[piece, :], squares[piece, :]
        high = square.astype(jnp.bfloat16).astype(jnp.float32)
        rest = LANES - 2 * (columns - main) - 2
        out_ref[:, :main] = own[:, :main].astype(jnp.bfloat16)
        out_ref[:, main : 2 * main] = more[:, :main].astype(jnp.bfloat16)
        out_ref[:, 2 * main :] = jnp.concatenate(
            [own[:, main:], more[:, main:], high, square - high, jnp.zeros((quarter, rest))],
            axis=1,
        ).astype(jnp.bfloat16)


def finish_kernel(depth, columns, where, *refs):
    refs = list(refs)
    part_refs = [refs.pop(0) for _ in range(4)]
    q_gain_ref, kv_gain_ref, cosine_ref, sine_ref, query_ref, cache_ref, parts = refs
    main = columns // LANES * LANES
    tail = columns - main
    for turn, ref in enumerate(part_refs):
        parts[where[turn]] = ref[...].astype(jnp.float32)
    added = {0: 1, 3: 2}
    pieces = []
    for plane in range(4):
        body, end = parts[plane, :, :main], parts[plane, :, 2 * main : 2 * main + tail]
        if plane in added:
            other = added[plane]
            body = body + parts[other, :, main : 2 * main]
            end = end + parts[other, :, 2 * main + tail : 2 * main + 2 * tail]
        pieces += [body, end]
    at = 2 * main + 2 * tail
    squares = parts[1, :, at : at + 1] + parts[1, :, at + 1 : at + 2]
    latent = jnp.concatenate(pieces, axis=1) * lax.rsqrt(squares / depth + epsilon)

    def normed(values, gain):
        mean_square = jnp.mean(values * values, axis=-1, keepdims=True)
        return (values * lax.rsqrt(mean_square + epsilon) * gain).astype(jnp.bfloat16)

    query_ref[...] = normed(latent[:, :QL], q_gain_ref[...])
    cache_ref[:, :KVL] = normed(latent[:, QL : QL + KVL], kv_gain_ref[...])
    half = ROPE // 2
    key = latent[:, QL + KVL :]
    turned = jnp.concatenate([key[:, half:], key[:, :half]], axis=1)
    cache_ref[:, KVL:] = (key * cosine_ref[...] + turned * sine_ref[...]).astype(jnp.bfloat16)


def on_device(hidden, attn_gain, q_gain, kv_gain, down_weight):
    row_count, width = hidden.shape
    ep, section, fsdp = lax.axis_size("ep"), lax.axis_size("section"), lax.axis_size("fsdp")
    assert ep == 4
    ep_index, section_index = lax.axis_index("ep"), lax.axis_index("section")
    fsdp_index = lax.axis_index("fsdp")
    quarter = row_count // ep
    rows = row_count // ROW_CHUNKS
    weight = down_weight.T
    columns = weight.shape[0]
    shared = fsdp == 2 and section == 4

    if shared:
        far = far_weight(weight, width)
    own = [hidden[i * rows : (i + 1) * rows] for i in range(ROW_CHUNKS)]
    up, down = [(0, 1), (1, 2), (2, 3)], [(3, 2), (2, 1), (1, 0)]
    rising = [lax.ppermute(block, "ep", up) for block in own]
    falling = [lax.ppermute(block, "ep", down) for block in own]
    rising_far = [lax.ppermute(block, "ep", up[1:]) for block in rising]
    falling_far = [lax.ppermute(block, "ep", down[1:]) for block in falling]
    if shared:
        pieces = other_weight(weight, width)
    else:
        weight = lax.all_gather(weight, "fsdp", axis=1, tiled=True)
        pieces = []
        block = lax.dynamic_slice(weight, (0, (3 - ep_index) * width), (columns, width))
        far = [lax.ppermute(block, "ep", [(0, 1), (3, 2)])]
    gain = attn_gain.reshape(1, -1)
    flat_pieces = [array for piece in pieces for array in piece]

    def place(block, valid):
        local = (block // 2 == fsdp_index) if shared else True
        inside = block % 2 if shared else block
        flips = [section_index ^ (2 * (block % 2) + half) for half in range(2)]
        fields = [valid, block, local, inside] + flips
        return [jnp.asarray(field).astype(jnp.int32) for field in fields]

    wheres = []
    for offset in (0, -1, 1):
        block = ep_index + offset
        wheres.append(jnp.stack(place(jnp.clip(block, 0, 3), (block >= 0) & (block < 4))))
    limits = pltpu.CompilerParams(vmem_limit_bytes=VMEM_LIMIT)
    total, squares = pl.pallas_call(
        functools.partial(near_kernel, 3, ROW_CHUNKS, len(pieces)),
        out_shape=(
            jax.ShapeDtypeStruct((row_count, columns), jnp.float32),
            jax.ShapeDtypeStruct((row_count, 1), jnp.float32),
        ),
        in_specs=[smem]
        + [anywhere] * (3 * ROW_CHUNKS)
        + [vmem]
        + [anywhere] * (1 + len(flat_pieces)),
        out_specs=(vmem, vmem),
        scratch_shapes=[
            pltpu.VMEM((3, row_count, width), jnp.bfloat16),
            pltpu.VMEM((3, columns, width), jnp.bfloat16),
            pltpu.SemaphoreType.DMA((3, ROW_CHUNKS)),
            pltpu.SemaphoreType.DMA((3, 4)),
        ],
        compiler_params=limits,
        cost_estimate=pl.CostEstimate(
            flops=6 * row_count * width * columns,
            bytes_accessed=6 * width * (row_count + columns),
            transcendentals=0,
        ),
    )(jnp.stack(wheres, axis=1), *own, *rising, *falling, gain, weight, *flat_pieces)

    far_block = ep_index ^ 2
    inner = ((ep_index == 1) | (ep_index == 2)).astype(jnp.int32)
    fields = place(far_block, (ep_index < 2)) + [inner, section_index]
    turns = jnp.stack([ep_index ^ turn for turn in range(4)])
    where = jnp.concatenate([jnp.stack([jnp.broadcast_to(f, (4,)) for f in fields]), turns[None]])
    main = columns // LANES * LANES
    message = jax.ShapeDtypeStruct((quarter, 2 * main + LANES), jnp.bfloat16)
    messages = pl.pallas_call(
        functools.partial(far_kernel, ROW_CHUNKS, len(pieces), len(far)),
        out_shape=(message,) * 4,
        in_specs=[smem]
        + [anywhere] * (2 * ROW_CHUNKS)
        + [vmem] * 3
        + [anywhere] * (1 + len(flat_pieces) + len(far)),
        out_specs=(vmem,) * 4,
        scratch_shapes=[
            pltpu.VMEM((row_count, columns), jnp.float32),
            pltpu.VMEM((row_count, columns), jnp.float32),
            pltpu.VMEM((row_count, 1), jnp.float32),
            pltpu.VMEM((row_count, width), jnp.bfloat16),
            pltpu.VMEM((columns, width), jnp.bfloat16),
            pltpu.VMEM((columns, width), jnp.bfloat16),
            pltpu.SemaphoreType.DMA((ROW_CHUNKS,)),
            pltpu.SemaphoreType.DMA((4,)),
            pltpu.SemaphoreType.DMA((4,)),
        ],
        compiler_params=limits,
        cost_estimate=pl.CostEstimate(
            flops=4 * row_count * width * columns,
            bytes_accessed=2 * width * (row_count + 2 * columns),
            transcendentals=0,
        ),
    )(
        where,
        *rising_far,
        *falling_far,
        gain,
        total,
        squares,
        weight,
        *flat_pieces,
        *far,
    )
    received = []
    for turn in range(4):
        moves = [
            (s * 4 + z, (s + 1) % section * 4 + (z ^ turn)) for s in range(section) for z in range(4)
        ]
        received.append(lax.ppermute(messages[turn], ("section", "ep"), moves))

    half = ROPE // 2
    position = (fsdp_index * row_count + ep_index * quarter + jnp.arange(quarter)) % LENGTH
    frequency = rope_base ** (-(jnp.arange(half).astype(jnp.float32) / half))
    angle = position.astype(jnp.float32)[:, None] * frequency[None, :]
    cosine, sine = jnp.cos(angle), jnp.sin(angle)
    return pl.pallas_call(
        functools.partial(finish_kernel, ep * width, columns),
        out_shape=(
            jax.ShapeDtypeStruct((quarter, QL), jnp.bfloat16),
            jax.ShapeDtypeStruct((quarter, KVL + ROPE), jnp.bfloat16),
        ),
        in_specs=[smem] + [vmem] * 8,
        out_specs=(vmem, vmem),
        scratch_shapes=[pltpu.VMEM((4, quarter, 2 * main + LANES), jnp.float32)],
        compiler_params=limits,
    )(
        turns,
        *received,
        q_gain.reshape(1, -1),
        kv_gain.reshape(1, -1),
        jnp.concatenate([cosine, cosine], axis=1),
        jnp.concatenate([-sine, sine], axis=1),
    )


def solution(mesh):
    placed = (P(("section", "fsdp"), "ep"), P(), P(), P(), P("fsdp", "ep"))
    return jax.shard_map(
        on_device,
        mesh=mesh,
        in_specs=placed,
        out_specs=(P(("section", "fsdp", "ep"), None), P(("section", "fsdp", "ep"), None)),
        check_vma=False,
    )
```

```python
import functools

import jax
import jax.numpy as jnp
import numpy as np
from jax import lax
from jax.experimental import pallas as pl
from jax.experimental.pallas import tpu as pltpu
from jax.sharding import PartitionSpec as P

QL = 1536
KVL = 512
ROPE = 64
LENGTH = 4096


epsilon = 1e-06
rope_base = 10000.0
CHUNKS = 2
PLANES = 4
NEAR_COST, LAST_COSTS = 15, (8, 2)
VMEM_LIMIT = 20 * 1024 * 1024

vmem = pl.BlockSpec(memory_space=pltpu.VMEM)
smem = pl.BlockSpec(memory_space=pltpu.SMEM)
anywhere = pl.BlockSpec(memory_space=pl.ANY)


def square_sums(values):
    return jnp.sum(values * values, axis=1, keepdims=True)


def product(gained, weight):
    return lax.dot_general(
        gained, weight, (((1,), (1,)), ((), ())), preferred_element_type=jnp.float32
    )


def near_kernel(chunks, sources, where, *refs):
    refs = list(refs)
    block_refs = [[refs.pop(0) for _ in range(chunks)] for _ in range(3)]
    gain_ref = refs.pop(0)
    source_refs = [refs.pop(0) for _ in range(sources)]
    total, squares, last_weight, blocks, weights, block_arrived, weight_arrived = refs
    rows, width = block_refs[0][0].shape

    def weight_copy(entry, act):
        into = weights.at[entry] if entry < 3 else last_weight
        for source, ref in enumerate(source_refs):

            @pl.when(where[1, entry] == source)
            def _():
                at = pl.multiple_of(where[2, entry] * width, width)
                copy = pltpu.make_async_copy(ref.at[:, pl.ds(at, width)], into, weight_arrived.at[entry])
                getattr(copy, act)()

    def block_copies(entry, act):
        for chunk, ref in enumerate(block_refs[entry]):
            into = blocks.at[entry, pl.ds(chunk * rows, rows)]
            copy = pltpu.make_async_copy(ref, into, block_arrived.at[entry, chunk])
            getattr(copy, act)()

    for entry in range(3):
        block_copies(entry, "start")
        weight_copy(entry, "start")
    weight_copy(3, "start")
    for entry in range(3):
        block_copies(entry, "wait")
        values = blocks[entry].astype(jnp.float32)
        at = pl.multiple_of(where[0, entry] * width, width)
        gained = (values * gain_ref[:, pl.ds(at, width)]).astype(jnp.bfloat16)
        weight_copy(entry, "wait")
        if entry == 0:
            squares[...] = square_sums(values)
            total[...] = product(gained, weights[entry])
        else:
            squares[...] += square_sums(values)
            total[...] += product(gained, weights[entry])
    weight_copy(3, "wait")


def last_kernel(first_row, depth, where, *refs):
    refs = list(refs)
    sides = [refs.pop(0) for _ in range(2)]
    gain_ref, weight_ref, total_ref, squares_ref = [refs.pop(0) for _ in range(4)]
    scaled = refs.pop(-1)
    rows, width = sides[0].shape
    values = jnp.where(where[3, 0] == 0, sides[0][...], sides[1][...]).astype(jnp.float32)
    squares = squares_ref[first_row : first_row + rows, :] + square_sums(values)
    at = pl.multiple_of(where[0, 3] * width, width)
    gained = (values * gain_ref[:, pl.ds(at, width)]).astype(jnp.bfloat16)
    total = total_ref[first_row : first_row + rows, :] + product(gained, weight_ref[...])
    scaled[...] = total * lax.rsqrt(squares / depth + epsilon)
    share = refs[0].shape[0]
    for turn, out_ref in enumerate(refs):
        at = pl.multiple_of(where[4, turn] * share, share)
        out_ref[...] = scaled[pl.ds(at, share), :].astype(jnp.bfloat16)


def finish_kernel(where, *refs):
    refs = list(refs)
    part_refs = [refs.pop(0) for _ in range(len(refs) - 7)]
    q_gain_ref, kv_gain_ref, cosine_ref, sine_ref, query_ref, cache_ref, parts = refs
    share = part_refs[0].shape[0]
    for index, ref in enumerate(part_refs):
        chunk, turn = index // PLANES, index % PLANES
        parts[where[4, turn], chunk * share : (chunk + 1) * share] = ref[...].astype(jnp.float32)
    latent = jnp.concatenate([parts[plane] for plane in range(PLANES)], axis=1)

    def normed(values, gain):
        mean_square = jnp.mean(values * values, axis=-1, keepdims=True)
        return (values * lax.rsqrt(mean_square + epsilon) * gain).astype(jnp.bfloat16)

    query_ref[...] = normed(latent[:, :QL], q_gain_ref[...])
    cache_ref[:, :KVL] = normed(latent[:, QL : QL + KVL], kv_gain_ref[...])
    half = ROPE // 2
    key = latent[:, QL + KVL :]
    turned = jnp.concatenate([key[:, half:], key[:, :half]], axis=1)
    cache_ref[:, KVL:] = (key * cosine_ref[...] + turned * sine_ref[...]).astype(jnp.bfloat16)


def tables(fsdp, shared):
    made = np.zeros((2, fsdp, PLANES, 5, PLANES), np.int32)
    per = PLANES // fsdp if shared else PLANES
    for core, y, z in np.ndindex(2, fsdp, PLANES):
        for column, block in enumerate((z, (z - 1) % PLANES, (z + 1) % PLANES, z ^ 2)):
            source, inside = 0, block % per
            if shared and block // per != y:
                source, inside = (1 if inside == core else 2), 0
            made[core, y, z, :4, column] = [block, source, inside, int(z < 2)]
        made[core, y, z, 4] = [z ^ turn for turn in range(PLANES)]
    return made


def on_device(hidden, attn_gain, q_gain, kv_gain, down_weight):
    row_count, width = hidden.shape
    section, fsdp = lax.axis_size("section"), lax.axis_size("fsdp")
    ep_index, fsdp_index = lax.axis_index("ep"), lax.axis_index("fsdp")
    assert lax.axis_size("ep") == PLANES
    quarter = row_count // PLANES
    share = quarter // CHUNKS
    rows = row_count // CHUNKS
    weight = down_weight.T
    columns = weight.shape[0]
    shared = fsdp == 2 and section % 2 == 0
    place = (lax.axis_index("section") % 2, fsdp_index, ep_index, 0, 0)
    where = lax.dynamic_slice(tables(fsdp, shared), place, (1, 1, 1, 5, PLANES)).reshape(5, PLANES)
    gain = attn_gain.reshape(1, -1)

    chunks = hidden.reshape(PLANES, CHUNKS, share, width)
    own = [chunks[:, chunk].reshape(rows, width) for chunk in range(CHUNKS)]
    up = [(z, (z + 1) % PLANES) for z in range(PLANES)]
    down = [(z, (z - 1) % PLANES) for z in range(PLANES)]
    below = [lax.ppermute(block, "ep", up) for block in own]
    above = [lax.ppermute(block, "ep", down) for block in own]
    if shared:
        core = lax.axis_index("section") % 2
        sent = lax.dynamic_slice(weight, (0, core * width), (columns, width))
        here = lax.ppermute(sent, "fsdp", [(0, 1), (1, 0)])
        below, above, here, where = lax.optimization_barrier((below, above, here, where))
        beside = lax.ppermute(here, "section", [(s, s ^ 1) for s in range(section)])
        sources = [weight, here, beside]
    else:
        sources = [lax.all_gather(weight, "fsdp", axis=1, tiled=True)]
    below_far = [lax.ppermute(block, "ep", [(1, 2), (2, 3)]) for block in below]
    above_far = [lax.ppermute(block, "ep", [(2, 1), (1, 0)]) for block in above]

    limits = pltpu.CompilerParams(vmem_limit_bytes=VMEM_LIMIT)

    def cost(microseconds):
        return pl.CostEstimate(
            flops=int(microseconds * 1.15e9), bytes_accessed=2 * row_count * width, transcendentals=0
        )

    total, squares, last_weight = pl.pallas_call(
        functools.partial(near_kernel, CHUNKS, len(sources)),
        out_shape=(
            jax.ShapeDtypeStruct((row_count, columns), jnp.float32),
            jax.ShapeDtypeStruct((row_count, 1), jnp.float32),
            jax.ShapeDtypeStruct((columns, width), jnp.bfloat16),
        ),
        in_specs=[smem] + [anywhere] * (3 * CHUNKS) + [vmem] + [anywhere] * len(sources),
        out_specs=(vmem, vmem, anywhere),
        scratch_shapes=[
            pltpu.VMEM((3, row_count, width), jnp.bfloat16),
            pltpu.VMEM((3, columns, width), jnp.bfloat16),
            pltpu.SemaphoreType.DMA((3, CHUNKS)),
            pltpu.SemaphoreType.DMA((4,)),
        ],
        compiler_params=limits,
        cost_estimate=cost(NEAR_COST),
    )(where, *own, *below, *above, gain, *sources)

    received = []
    for chunk in range(CHUNKS):
        messages = pl.pallas_call(
            functools.partial(last_kernel, chunk * rows, PLANES * width),
            out_shape=(jax.ShapeDtypeStruct((share, columns), jnp.bfloat16),) * PLANES,
            in_specs=[smem] + [vmem] * 6,
            out_specs=(vmem,) * PLANES,
            scratch_shapes=[pltpu.VMEM((rows, columns), jnp.float32)],
            compiler_params=limits,
            cost_estimate=cost(LAST_COSTS[chunk]),
        )(where, below_far[chunk], above_far[chunk], gain, last_weight, total, squares)
        for turn in range(PLANES):
            moves = [
                (s * PLANES + z, (s + 1) % section * PLANES + (z ^ turn))
                for s in range(section)
                for z in range(PLANES)
            ]
            received.append(lax.ppermute(messages[turn], ("section", "ep"), moves))

    half = ROPE // 2
    position = (fsdp_index * row_count + ep_index * quarter + jnp.arange(quarter)) % LENGTH
    frequency = rope_base ** (-(jnp.arange(half).astype(jnp.float32) / half))
    angle = position.astype(jnp.float32)[:, None] * frequency[None, :]
    cosine, sine = jnp.cos(angle), jnp.sin(angle)
    return pl.pallas_call(
        finish_kernel,
        out_shape=(
            jax.ShapeDtypeStruct((quarter, QL), jnp.bfloat16),
            jax.ShapeDtypeStruct((quarter, KVL + ROPE), jnp.bfloat16),
        ),
        in_specs=[smem] + [vmem] * (len(received) + 4),
        out_specs=(vmem, vmem),
        scratch_shapes=[pltpu.VMEM((PLANES, quarter, columns), jnp.float32)],
        compiler_params=limits,
    )(
        where,
        *received,
        q_gain.reshape(1, -1),
        kv_gain.reshape(1, -1),
        jnp.concatenate([cosine, cosine], axis=1),
        jnp.concatenate([-sine, sine], axis=1),
    )


def solution(mesh):
    placed = (P(("section", "fsdp"), "ep"), P(), P(), P(), P("fsdp", "ep"))
    return jax.shard_map(
        on_device,
        mesh=mesh,
        in_specs=placed,
        out_specs=(P(("section", "fsdp", "ep"), None), P(("section", "fsdp", "ep"), None)),
        check_vma=False,
    )
```

```python
import functools

import jax
import jax.numpy as jnp
import numpy as np
from jax import lax
from jax.experimental import pallas as pl
from jax.experimental.pallas import tpu as pltpu
from jax.sharding import PartitionSpec as P

QL = 1536
KVL = 512
ROPE = 64
LENGTH = 4096


epsilon = 1e-06
rope_base = 10000.0
CHUNKS = 1
PLANES = 4
PARTS = 3
NEAR_COST, LAST_COSTS = 1, (2, 2)
VMEM_LIMIT = 20 * 1024 * 1024

vmem = pl.BlockSpec(memory_space=pltpu.VMEM)
smem = pl.BlockSpec(memory_space=pltpu.SMEM)
anywhere = pl.BlockSpec(memory_space=pl.ANY)


def square_sums(values):
    return jnp.sum(values * values, axis=1, keepdims=True)


def product(gained, weight):
    return lax.dot_general(
        gained, weight, (((1,), (1,)), ((), ())), preferred_element_type=jnp.float32
    )


def near_kernel(chunks, layout, where, *refs):
    refs = list(refs)
    block_refs = [[refs.pop(0) for _ in range(chunks)] for _ in range(3)]
    gain_ref = refs.pop(0)
    source_refs = [[refs.pop(0) for _ in range(parts)] for parts in layout]
    total, squares, last_weight, blocks, weights, block_arrived, weight_arrived = refs
    rows, width = block_refs[0][0].shape

    def weight_copy(entry, act):
        into = weights.at[entry] if entry < 3 else last_weight
        for source, parts in enumerate(source_refs):

            @pl.when(where[1, entry] == source)
            def _():
                at = pl.multiple_of(where[2, entry] * width, width)
                for part, ref in enumerate(parts):
                    height = ref.shape[0]
                    copy = pltpu.make_async_copy(
                        ref.at[:, pl.ds(at, width)],
                        into.at[pl.ds(part * height, height)],
                        weight_arrived.at[entry, part],
                    )
                    getattr(copy, act)()

    def block_copies(entry, act):
        for chunk, ref in enumerate(block_refs[entry]):
            into = blocks.at[entry, pl.ds(chunk * rows, rows)]
            copy = pltpu.make_async_copy(ref, into, block_arrived.at[entry, chunk])
            getattr(copy, act)()

    for entry in range(3):
        block_copies(entry, "start")
        weight_copy(entry, "start")
    weight_copy(3, "start")
    for entry in range(3):
        block_copies(entry, "wait")
        values = blocks[entry].astype(jnp.float32)
        at = pl.multiple_of(where[0, entry] * width, width)
        gained = (values * gain_ref[:, pl.ds(at, width)]).astype(jnp.bfloat16)
        weight_copy(entry, "wait")
        if entry == 0:
            squares[...] = square_sums(values)
            total[...] = product(gained, weights[entry])
        else:
            squares[...] += square_sums(values)
            total[...] += product(gained, weights[entry])
    weight_copy(3, "wait")


def last_kernel(first_row, depth, where, *refs):
    refs = list(refs)
    sides = [refs.pop(0) for _ in range(2)]
    gain_ref, weight_ref, total_ref, squares_ref = [refs.pop(0) for _ in range(4)]
    scaled = refs.pop(-1)
    rows, width = sides[0].shape
    values = jnp.where(where[3, 0] == 0, sides[0][...], sides[1][...]).astype(jnp.float32)
    squares = squares_ref[first_row : first_row + rows, :] + square_sums(values)
    at = pl.multiple_of(where[0, 3] * width, width)
    gained = (values * gain_ref[:, pl.ds(at, width)]).astype(jnp.bfloat16)
    total = total_ref[first_row : first_row + rows, :] + product(gained, weight_ref[...])
    scaled[...] = total * lax.rsqrt(squares / depth + epsilon)
    share = refs[0].shape[0]
    for turn, out_ref in enumerate(refs):
        at = pl.multiple_of(where[4, turn] * share, share)
        out_ref[...] = scaled[pl.ds(at, share), :].astype(jnp.bfloat16)


def finish_kernel(where, *refs):
    refs = list(refs)
    part_refs = [refs.pop(0) for _ in range(len(refs) - 7)]
    q_gain_ref, kv_gain_ref, cosine_ref, sine_ref, query_ref, cache_ref, parts = refs
    share = part_refs[0].shape[0]
    for index, ref in enumerate(part_refs):
        chunk, turn = index // PLANES, index % PLANES
        parts[where[4, turn], chunk * share : (chunk + 1) * share] = ref[...].astype(jnp.float32)
    latent = jnp.concatenate([parts[plane] for plane in range(PLANES)], axis=1)

    def normed(values, gain):
        mean_square = jnp.mean(values * values, axis=-1, keepdims=True)
        return (values * lax.rsqrt(mean_square + epsilon) * gain).astype(jnp.bfloat16)

    query_ref[...] = normed(latent[:, :QL], q_gain_ref[...])
    cache_ref[:, :KVL] = normed(latent[:, QL : QL + KVL], kv_gain_ref[...])
    half = ROPE // 2
    key = latent[:, QL + KVL :]
    turned = jnp.concatenate([key[:, half:], key[:, :half]], axis=1)
    cache_ref[:, KVL:] = (key * cosine_ref[...] + turned * sine_ref[...]).astype(jnp.bfloat16)


def tables(fsdp, shared):
    made = np.zeros((2, fsdp, PLANES, 5, PLANES), np.int32)
    per = PLANES // fsdp if shared else PLANES
    for core, y, z in np.ndindex(2, fsdp, PLANES):
        for column, block in enumerate((z, (z - 1) % PLANES, (z + 1) % PLANES, z ^ 2)):
            source, inside = 0, block % per
            if shared and block // per != y:
                source, inside = (1 if inside == core else 2), 0
            made[core, y, z, :4, column] = [block, source, inside, int(z < 2)]
        made[core, y, z, 4] = [z ^ turn for turn in range(PLANES)]
    return made


def on_device(hidden, attn_gain, q_gain, kv_gain, down_weight):
    row_count, width = hidden.shape
    section, fsdp = lax.axis_size("section"), lax.axis_size("fsdp")
    ep_index, fsdp_index = lax.axis_index("ep"), lax.axis_index("fsdp")
    assert lax.axis_size("ep") == PLANES
    quarter = row_count // PLANES
    share = quarter // CHUNKS
    rows = row_count // CHUNKS
    weight = down_weight.T
    columns = weight.shape[0]
    shared = fsdp == 2 and section % 2 == 0
    place = (lax.axis_index("section") % 2, fsdp_index, ep_index, 0, 0)
    where = lax.dynamic_slice(tables(fsdp, shared), place, (1, 1, 1, 5, PLANES)).reshape(5, PLANES)
    gain = attn_gain.reshape(1, -1)

    chunks = hidden.reshape(PLANES, CHUNKS, share, width)
    own = [chunks[:, chunk].reshape(rows, width) for chunk in range(CHUNKS)]
    up = [(z, (z + 1) % PLANES) for z in range(PLANES)]
    down = [(z, (z - 1) % PLANES) for z in range(PLANES)]
    below = [lax.ppermute(block, "ep", up) for block in own]
    above = [lax.ppermute(block, "ep", down) for block in own]
    if shared:
        core = lax.axis_index("section") % 2
        height = columns // PARTS
        here = [
            lax.dynamic_slice(weight, (part * height, core * width), (height, width))
            for part in range(PARTS)
        ]
        here = [lax.ppermute(part, "fsdp", [(0, 1), (1, 0)]) for part in here]
        cores = [(s, s ^ 1) for s in range(section)]
        sources = [[weight], here, [lax.ppermute(part, "section", cores) for part in here]]
    else:
        sources = [[lax.all_gather(weight, "fsdp", axis=1, tiled=True)]]
    below_far = [lax.ppermute(block, "ep", [(1, 2), (2, 3)]) for block in below]
    above_far = [lax.ppermute(block, "ep", [(2, 1), (1, 0)]) for block in above]

    limits = pltpu.CompilerParams(vmem_limit_bytes=VMEM_LIMIT)

    def cost(microseconds):
        return pl.CostEstimate(
            flops=int(microseconds * 1.15e9), bytes_accessed=2 * row_count * width, transcendentals=0
        )

    total, squares, last_weight = pl.pallas_call(
        functools.partial(near_kernel, CHUNKS, [len(parts) for parts in sources]),
        out_shape=(
            jax.ShapeDtypeStruct((row_count, columns), jnp.float32),
            jax.ShapeDtypeStruct((row_count, 1), jnp.float32),
            jax.ShapeDtypeStruct((columns, width), jnp.bfloat16),
        ),
        in_specs=[smem] + [anywhere] * (3 * CHUNKS) + [vmem] + [anywhere] * sum(len(parts) for parts in sources),
        out_specs=(vmem, vmem, anywhere),
        scratch_shapes=[
            pltpu.VMEM((3, row_count, width), jnp.bfloat16),
            pltpu.VMEM((3, columns, width), jnp.bfloat16),
            pltpu.SemaphoreType.DMA((3, CHUNKS)),
            pltpu.SemaphoreType.DMA((4, PARTS)),
        ],
        compiler_params=limits,
        cost_estimate=cost(NEAR_COST),
    )(where, *own, *below, *above, gain, *[part for parts in sources for part in parts])

    received = []
    for chunk in range(CHUNKS):
        messages = pl.pallas_call(
            functools.partial(last_kernel, chunk * rows, PLANES * width),
            out_shape=(jax.ShapeDtypeStruct((share, columns), jnp.bfloat16),) * PLANES,
            in_specs=[smem] + [vmem] * 6,
            out_specs=(vmem,) * PLANES,
            scratch_shapes=[pltpu.VMEM((rows, columns), jnp.float32)],
            compiler_params=limits,
            cost_estimate=cost(LAST_COSTS[chunk]),
        )(where, below_far[chunk], above_far[chunk], gain, last_weight, total, squares)
        for turn in range(PLANES):
            moves = [
                (s * PLANES + z, (s + 1) % section * PLANES + (z ^ turn))
                for s in range(section)
                for z in range(PLANES)
            ]
            received.append(lax.ppermute(messages[turn], ("section", "ep"), moves))

    half = ROPE // 2
    position = (fsdp_index * row_count + ep_index * quarter + jnp.arange(quarter)) % LENGTH
    frequency = rope_base ** (-(jnp.arange(half).astype(jnp.float32) / half))
    angle = position.astype(jnp.float32)[:, None] * frequency[None, :]
    cosine, sine = jnp.cos(angle), jnp.sin(angle)
    return pl.pallas_call(
        finish_kernel,
        out_shape=(
            jax.ShapeDtypeStruct((quarter, QL), jnp.bfloat16),
            jax.ShapeDtypeStruct((quarter, KVL + ROPE), jnp.bfloat16),
        ),
        in_specs=[smem] + [vmem] * (len(received) + 4),
        out_specs=(vmem, vmem),
        scratch_shapes=[pltpu.VMEM((PLANES, quarter, columns), jnp.float32)],
        compiler_params=limits,
    )(
        where,
        *received,
        q_gain.reshape(1, -1),
        kv_gain.reshape(1, -1),
        jnp.concatenate([cosine, cosine], axis=1),
        jnp.concatenate([-sine, sine], axis=1),
    )


def solution(mesh):
    placed = (P(("section", "fsdp"), "ep"), P(), P(), P(), P("fsdp", "ep"))
    return jax.shard_map(
        on_device,
        mesh=mesh,
        in_specs=placed,
        out_specs=(P(("section", "fsdp", "ep"), None), P(("section", "fsdp", "ep"), None)),
        check_vma=False,
    )
```

```python
import functools

import jax
import jax.numpy as jnp
import numpy as np
from jax import lax
from jax.experimental import pallas as pl
from jax.experimental.pallas import tpu as pltpu
from jax.sharding import PartitionSpec as P

QL = 1536
KVL = 512
ROPE = 64
LENGTH = 4096


epsilon = 1e-06
rope_base = 10000.0
CHUNKS = 1
PLANES = 4
PARTS = 3
NEAR_COST, LAST_COSTS = 1, (2, 2)
VMEM_LIMIT = 20 * 1024 * 1024

vmem = pl.BlockSpec(memory_space=pltpu.VMEM)
smem = pl.BlockSpec(memory_space=pltpu.SMEM)
anywhere = pl.BlockSpec(memory_space=pl.ANY)


def square_sums(values):
    return jnp.sum(values * values, axis=1, keepdims=True)


def product(gained, weight):
    return lax.dot_general(
        gained, weight, (((1,), (1,)), ((), ())), preferred_element_type=jnp.float32
    )


def near_kernel(chunks, layout, where, *refs):
    refs = list(refs)
    block_refs = [[refs.pop(0) for _ in range(chunks)] for _ in range(3)]
    gain_ref = refs.pop(0)
    source_refs = [[refs.pop(0) for _ in range(parts)] for parts in layout]
    total, squares, last_weight, blocks, weights, block_arrived, weight_arrived = refs
    rows, width = block_refs[0][0].shape

    def weight_copy(entry, act):
        into = weights.at[entry] if entry < 3 else last_weight
        for source, parts in enumerate(source_refs):

            @pl.when(where[1, entry] == source)
            def _():
                at = pl.multiple_of(where[2, entry] * width, width)
                for part, ref in enumerate(parts):
                    height = ref.shape[0]
                    copy = pltpu.make_async_copy(
                        ref.at[:, pl.ds(at, width)],
                        into.at[pl.ds(part * height, height)],
                        weight_arrived.at[entry, part],
                    )
                    getattr(copy, act)()

    def block_copies(entry, act):
        for chunk, ref in enumerate(block_refs[entry]):
            into = blocks.at[entry, pl.ds(chunk * rows, rows)]
            copy = pltpu.make_async_copy(ref, into, block_arrived.at[entry, chunk])
            getattr(copy, act)()

    for entry in range(3):
        block_copies(entry, "start")
        weight_copy(entry, "start")
    weight_copy(3, "start")
    for entry in range(3):
        block_copies(entry, "wait")
        values = blocks[entry].astype(jnp.float32)
        at = pl.multiple_of(where[0, entry] * width, width)
        gained = (values * gain_ref[:, pl.ds(at, width)]).astype(jnp.bfloat16)
        weight_copy(entry, "wait")
        if entry == 0:
            squares[...] = square_sums(values)
            total[...] = product(gained, weights[entry])
        else:
            squares[...] += square_sums(values)
            total[...] += product(gained, weights[entry])
    weight_copy(3, "wait")


def last_kernel(first_row, depth, where, *refs):
    refs = list(refs)
    sides = [refs.pop(0) for _ in range(2)]
    gain_ref, weight_ref, total_ref, squares_ref = [refs.pop(0) for _ in range(4)]
    scaled = refs.pop(-1)
    rows, width = sides[0].shape
    values = jnp.where(where[3, 0] == 0, sides[0][...], sides[1][...]).astype(jnp.float32)
    squares = squares_ref[first_row : first_row + rows, :] + square_sums(values)
    at = pl.multiple_of(where[0, 3] * width, width)
    gained = (values * gain_ref[:, pl.ds(at, width)]).astype(jnp.bfloat16)
    total = total_ref[first_row : first_row + rows, :] + product(gained, weight_ref[...])
    scaled[...] = total * lax.rsqrt(squares / depth + epsilon)
    share = refs[0].shape[0]
    for turn, out_ref in enumerate(refs):
        at = pl.multiple_of(where[4, turn] * share, share)
        out_ref[...] = scaled[pl.ds(at, share), :].astype(jnp.bfloat16)


def finish_kernel(where, *refs):
    refs = list(refs)
    part_refs = [refs.pop(0) for _ in range(len(refs) - 7)]
    q_gain_ref, kv_gain_ref, cosine_ref, sine_ref, query_ref, cache_ref, parts = refs
    share = part_refs[0].shape[0]
    for index, ref in enumerate(part_refs):
        chunk, turn = index // PLANES, PLANES - 1 - index % PLANES
        parts[where[4, turn], chunk * share : (chunk + 1) * share] = ref[...].astype(jnp.float32)
    latent = jnp.concatenate([parts[plane] for plane in range(PLANES)], axis=1)

    def normed(values, gain):
        mean_square = jnp.mean(values * values, axis=-1, keepdims=True)
        return (values * lax.rsqrt(mean_square + epsilon) * gain).astype(jnp.bfloat16)

    query_ref[...] = normed(latent[:, :QL], q_gain_ref[...])
    cache_ref[:, :KVL] = normed(latent[:, QL : QL + KVL], kv_gain_ref[...])
    half = ROPE // 2
    key = latent[:, QL + KVL :]
    turned = jnp.concatenate([key[:, half:], key[:, :half]], axis=1)
    cache_ref[:, KVL:] = (key * cosine_ref[...] + turned * sine_ref[...]).astype(jnp.bfloat16)


def tables(fsdp, shared):
    made = np.zeros((2, fsdp, PLANES, 5, PLANES), np.int32)
    per = PLANES // fsdp if shared else PLANES
    for core, y, z in np.ndindex(2, fsdp, PLANES):
        for column, block in enumerate((z, (z - 1) % PLANES, (z + 1) % PLANES, z ^ 2)):
            source, inside = 0, block % per
            if shared and block // per != y:
                source, inside = (1 if inside == core else 2), 0
            made[core, y, z, :4, column] = [block, source, inside, int(z < 2)]
        made[core, y, z, 4] = [z ^ turn for turn in range(PLANES)]
    return made


def on_device(hidden, attn_gain, q_gain, kv_gain, down_weight):
    row_count, width = hidden.shape
    section, fsdp = lax.axis_size("section"), lax.axis_size("fsdp")
    ep_index, fsdp_index = lax.axis_index("ep"), lax.axis_index("fsdp")
    assert lax.axis_size("ep") == PLANES
    quarter = row_count // PLANES
    share = quarter // CHUNKS
    rows = row_count // CHUNKS
    weight = down_weight.T
    columns = weight.shape[0]
    shared = fsdp == 2 and section % 2 == 0
    place = (lax.axis_index("section") % 2, fsdp_index, ep_index, 0, 0)
    where = lax.dynamic_slice(tables(fsdp, shared), place, (1, 1, 1, 5, PLANES)).reshape(5, PLANES)
    gain = attn_gain.reshape(1, -1)

    chunks = hidden.reshape(PLANES, CHUNKS, share, width)
    own = [chunks[:, chunk].reshape(rows, width) for chunk in range(CHUNKS)]
    up = [(z, (z + 1) % PLANES) for z in range(PLANES)]
    down = [(z, (z - 1) % PLANES) for z in range(PLANES)]
    below = [lax.ppermute(block, "ep", up) for block in own]
    above = [lax.ppermute(block, "ep", down) for block in own]
    if shared:
        core = lax.axis_index("section") % 2
        height = columns // PARTS
        here = [
            lax.dynamic_slice(weight, (part * height, core * width), (height, width))
            for part in range(PARTS)
        ]
        here = [lax.ppermute(part, "fsdp", [(0, 1), (1, 0)]) for part in here]
        cores = [(s, s ^ 1) for s in range(section)]
        sources = [[weight], here, [lax.ppermute(part, "section", cores) for part in here]]
    else:
        sources = [[lax.all_gather(weight, "fsdp", axis=1, tiled=True)]]
    below_far = [lax.ppermute(block, "ep", [(1, 2), (2, 3)]) for block in below]
    above_far = [lax.ppermute(block, "ep", [(2, 1), (1, 0)]) for block in above]

    limits = pltpu.CompilerParams(vmem_limit_bytes=VMEM_LIMIT)

    def cost(microseconds):
        return pl.CostEstimate(
            flops=int(microseconds * 1.15e9), bytes_accessed=2 * row_count * width, transcendentals=0
        )

    total, squares, last_weight = pl.pallas_call(
        functools.partial(near_kernel, CHUNKS, [len(parts) for parts in sources]),
        out_shape=(
            jax.ShapeDtypeStruct((row_count, columns), jnp.float32),
            jax.ShapeDtypeStruct((row_count, 1), jnp.float32),
            jax.ShapeDtypeStruct((columns, width), jnp.bfloat16),
        ),
        in_specs=[smem] + [anywhere] * (3 * CHUNKS) + [vmem] + [anywhere] * sum(len(parts) for parts in sources),
        out_specs=(vmem, vmem, anywhere),
        scratch_shapes=[
            pltpu.VMEM((3, row_count, width), jnp.bfloat16),
            pltpu.VMEM((3, columns, width), jnp.bfloat16),
            pltpu.SemaphoreType.DMA((3, CHUNKS)),
            pltpu.SemaphoreType.DMA((4, PARTS)),
        ],
        compiler_params=limits,
        cost_estimate=cost(NEAR_COST),
    )(where, *own, *below, *above, gain, *[part for parts in sources for part in parts])

    received = []
    for chunk in range(CHUNKS):
        messages = pl.pallas_call(
            functools.partial(last_kernel, chunk * rows, PLANES * width),
            out_shape=(jax.ShapeDtypeStruct((share, columns), jnp.bfloat16),) * PLANES,
            in_specs=[smem] + [vmem] * 6,
            out_specs=(vmem,) * PLANES,
            scratch_shapes=[pltpu.VMEM((rows, columns), jnp.float32)],
            compiler_params=limits,
            cost_estimate=cost(LAST_COSTS[chunk]),
        )(where, below_far[chunk], above_far[chunk], gain, last_weight, total, squares)
        arrived = {}
        for turn in reversed(range(PLANES)):
            moves = [
                (s * PLANES + z, (s + 1) % section * PLANES + (z ^ turn))
                for s in range(section)
                for z in range(PLANES)
            ]
            arrived[turn] = lax.ppermute(messages[turn], ("section", "ep"), moves)
        received += list(arrived.values())

    half = ROPE // 2
    position = (fsdp_index * row_count + ep_index * quarter + jnp.arange(quarter)) % LENGTH
    frequency = rope_base ** (-(jnp.arange(half).astype(jnp.float32) / half))
    angle = position.astype(jnp.float32)[:, None] * frequency[None, :]
    cosine, sine = jnp.cos(angle), jnp.sin(angle)
    return pl.pallas_call(
        finish_kernel,
        out_shape=(
            jax.ShapeDtypeStruct((quarter, QL), jnp.bfloat16),
            jax.ShapeDtypeStruct((quarter, KVL + ROPE), jnp.bfloat16),
        ),
        in_specs=[smem] + [vmem] * (len(received) + 4),
        out_specs=(vmem, vmem),
        scratch_shapes=[pltpu.VMEM((PLANES, quarter, columns), jnp.float32)],
        compiler_params=limits,
    )(
        where,
        *received,
        q_gain.reshape(1, -1),
        kv_gain.reshape(1, -1),
        jnp.concatenate([cosine, cosine], axis=1),
        jnp.concatenate([-sine, sine], axis=1),
    )


def solution(mesh):
    placed = (P(("section", "fsdp"), "ep"), P(), P(), P(), P("fsdp", "ep"))
    return jax.shard_map(
        on_device,
        mesh=mesh,
        in_specs=placed,
        out_specs=(P(("section", "fsdp", "ep"), None), P(("section", "fsdp", "ep"), None)),
        check_vma=False,
    )
```

```python
import functools

import jax
import jax.numpy as jnp
import numpy as np
from jax import lax
from jax.experimental import pallas as pl
from jax.experimental.pallas import tpu as pltpu
from jax.sharding import PartitionSpec as P

QL = 1536
KVL = 512
ROPE = 64
LENGTH = 4096


epsilon = 1e-06
rope_base = 10000.0
PLANES = 4
PARTS = 3
NEAR_COST, LAST_COST = 1, 2
TURNS = 3, 2, 1, 0
VMEM_LIMIT = 20 * 1024 * 1024

vmem = pl.BlockSpec(memory_space=pltpu.VMEM)
smem = pl.BlockSpec(memory_space=pltpu.SMEM)
anywhere = pl.BlockSpec(memory_space=pl.ANY)


def square_sums(values):
    return jnp.sum(values * values, axis=1, keepdims=True)


def product(gained, weight):
    return lax.dot_general(
        gained, weight, (((1,), (1,)), ((), ())), preferred_element_type=jnp.float32
    )


def near_kernel(layout, where, *refs):
    refs = list(refs)
    block_refs = [refs.pop(0) for _ in range(3)]
    gain_ref = refs.pop(0)
    source_refs = [[refs.pop(0) for _ in range(parts)] for parts in layout]
    total, squares, last_weight, blocks, weights, block_arrived, weight_arrived = refs
    width = blocks.shape[2]

    def weight_copy(entry, act):
        into = weights.at[entry] if entry < 3 else last_weight
        for source, parts in enumerate(source_refs):

            @pl.when(where[1, entry] == source)
            def _():
                at = pl.multiple_of(where[2, entry] * width, width)
                for part, ref in enumerate(parts):
                    height = ref.shape[0]
                    copy = pltpu.make_async_copy(
                        ref.at[:, pl.ds(at, width)],
                        into.at[pl.ds(part * height, height)],
                        weight_arrived.at[entry, part],
                    )
                    getattr(copy, act)()

    def block_copy(entry, act):
        copy = pltpu.make_async_copy(block_refs[entry], blocks.at[entry], block_arrived.at[entry])
        getattr(copy, act)()

    for entry in range(3):
        block_copy(entry, "start")
        weight_copy(entry, "start")
    weight_copy(3, "start")
    for entry in range(3):
        block_copy(entry, "wait")
        values = blocks[entry].astype(jnp.float32)
        at = pl.multiple_of(where[0, entry] * width, width)
        gained = (values * gain_ref[:, pl.ds(at, width)]).astype(jnp.bfloat16)
        weight_copy(entry, "wait")
        if entry == 0:
            squares[...] = square_sums(values)
            total[...] = product(gained, weights[entry])
        else:
            squares[...] += square_sums(values)
            total[...] += product(gained, weights[entry])
    weight_copy(3, "wait")


def last_kernel(depth, where, *refs):
    refs = list(refs)
    block_ref, gain_ref, weight_ref, total_ref, squares_ref = [refs.pop(0) for _ in range(5)]
    scaled = refs.pop(-1)
    width = block_ref.shape[1]
    values = block_ref[...].astype(jnp.float32)
    squares = squares_ref[...] + square_sums(values)
    at = pl.multiple_of(where[0, 3] * width, width)
    gained = (values * gain_ref[:, pl.ds(at, width)]).astype(jnp.bfloat16)
    total = total_ref[...] + product(gained, weight_ref[...])
    scaled[...] = total * lax.rsqrt(squares / depth + epsilon)
    quarter = refs[0].shape[0]
    for turn, out_ref in zip(TURNS, refs):
        at = pl.multiple_of(where[3, turn] * quarter, quarter)
        out_ref[...] = scaled[pl.ds(at, quarter), :].astype(jnp.bfloat16)


def finish_kernel(where, *refs):
    refs = list(refs)
    part_refs = [refs.pop(0) for _ in range(len(refs) - 7)]
    q_gain_ref, kv_gain_ref, cosine_ref, sine_ref, query_ref, cache_ref, parts = refs
    for turn, ref in zip(TURNS, part_refs):
        parts[where[3, turn]] = ref[...].astype(jnp.float32)
    latent = jnp.concatenate([parts[plane] for plane in range(PLANES)], axis=1)

    def normed(values, gain):
        mean_square = jnp.mean(values * values, axis=-1, keepdims=True)
        return (values * lax.rsqrt(mean_square + epsilon) * gain).astype(jnp.bfloat16)

    query_ref[...] = normed(latent[:, :QL], q_gain_ref[...])
    cache_ref[:, :KVL] = normed(latent[:, QL : QL + KVL], kv_gain_ref[...])
    half = ROPE // 2
    key = latent[:, QL + KVL :]
    turned = jnp.concatenate([key[:, half:], key[:, :half]], axis=1)
    cache_ref[:, KVL:] = (key * cosine_ref[...] + turned * sine_ref[...]).astype(jnp.bfloat16)


def tables(fsdp, shared):
    made = np.zeros((2, fsdp, PLANES, 4, PLANES), np.int32)
    per = PLANES // fsdp if shared else PLANES
    for core, y, z in np.ndindex(2, fsdp, PLANES):
        for column, block in enumerate((z, PLANES - 1 - z, z ^ 1, z ^ 2)):
            source, inside = 0, block % per
            if shared and block // per != y:
                source, inside = (1 if inside == core else 2), 0
            made[core, y, z, :3, column] = [block, source, inside]
        made[core, y, z, 3] = [z ^ turn for turn in range(PLANES)]
    return made


def on_device(hidden, attn_gain, q_gain, kv_gain, down_weight):
    row_count, width = hidden.shape
    section, fsdp = lax.axis_size("section"), lax.axis_size("fsdp")
    ep_index, fsdp_index = lax.axis_index("ep"), lax.axis_index("fsdp")
    assert lax.axis_size("ep") == PLANES
    quarter = row_count // PLANES
    weight = down_weight.T
    columns = weight.shape[0]
    shared = fsdp == 2 and section % 2 == 0
    place = (lax.axis_index("section") % 2, fsdp_index, ep_index, 0, 0)
    where = lax.dynamic_slice(tables(fsdp, shared), place, (1, 1, 1, 4, PLANES)).reshape(4, PLANES)
    gain = attn_gain.reshape(1, -1)

    mirrored = lax.ppermute(hidden, "ep", [(z, PLANES - 1 - z) for z in range(PLANES)])
    paired = lax.ppermute(hidden, "ep", [(z, z ^ 1) for z in range(PLANES)])
    if shared:
        core = lax.axis_index("section") % 2
        height = columns // PARTS
        here = [
            lax.dynamic_slice(weight, (part * height, core * width), (height, width))
            for part in range(PARTS)
        ]
        here = [lax.ppermute(part, "fsdp", [(0, 1), (1, 0)]) for part in here]
        cores = [(s, s ^ 1) for s in range(section)]
        sources = [[weight], here, [lax.ppermute(part, "section", cores) for part in here]]
    else:
        sources = [[lax.all_gather(weight, "fsdp", axis=1, tiled=True)]]
    far = lax.ppermute(mirrored, "ep", [(z, z ^ 1) for z in range(PLANES)])

    limits = pltpu.CompilerParams(vmem_limit_bytes=VMEM_LIMIT)

    def cost(microseconds):
        return pl.CostEstimate(
            flops=int(microseconds * 1.15e9), bytes_accessed=2 * row_count * width, transcendentals=0
        )

    total, squares, last_weight = pl.pallas_call(
        functools.partial(near_kernel, [len(parts) for parts in sources]),
        out_shape=(
            jax.ShapeDtypeStruct((row_count, columns), jnp.float32),
            jax.ShapeDtypeStruct((row_count, 1), jnp.float32),
            jax.ShapeDtypeStruct((columns, width), jnp.bfloat16),
        ),
        in_specs=[smem] + [anywhere] * 3 + [vmem] + [anywhere] * sum(len(parts) for parts in sources),
        out_specs=(vmem, vmem, anywhere),
        scratch_shapes=[
            pltpu.VMEM((3, row_count, width), jnp.bfloat16),
            pltpu.VMEM((3, columns, width), jnp.bfloat16),
            pltpu.SemaphoreType.DMA((3,)),
            pltpu.SemaphoreType.DMA((4, PARTS)),
        ],
        compiler_params=limits,
        cost_estimate=cost(NEAR_COST),
    )(where, hidden, mirrored, paired, gain, *[part for parts in sources for part in parts])

    messages = pl.pallas_call(
        functools.partial(last_kernel, PLANES * width),
        out_shape=(jax.ShapeDtypeStruct((quarter, columns), jnp.bfloat16),) * PLANES,
        in_specs=[smem] + [vmem] * 5,
        out_specs=(vmem,) * PLANES,
        scratch_shapes=[pltpu.VMEM((row_count, columns), jnp.float32)],
        compiler_params=limits,
        cost_estimate=cost(LAST_COST),
    )(where, far, gain, last_weight, total, squares)
    received = []
    for turn, message in zip(TURNS, messages):
        moves = [
            (s * PLANES + z, (s + 1) % section * PLANES + (z ^ turn))
            for s in range(section)
            for z in range(PLANES)
        ]
        received.append(lax.ppermute(message, ("section", "ep"), moves))

    half = ROPE // 2
    position = (fsdp_index * row_count + ep_index * quarter + jnp.arange(quarter)) % LENGTH
    frequency = rope_base ** (-(jnp.arange(half).astype(jnp.float32) / half))
    angle = position.astype(jnp.float32)[:, None] * frequency[None, :]
    cosine, sine = jnp.cos(angle), jnp.sin(angle)
    return pl.pallas_call(
        finish_kernel,
        out_shape=(
            jax.ShapeDtypeStruct((quarter, QL), jnp.bfloat16),
            jax.ShapeDtypeStruct((quarter, KVL + ROPE), jnp.bfloat16),
        ),
        in_specs=[smem] + [vmem] * (len(received) + 4),
        out_specs=(vmem, vmem),
        scratch_shapes=[pltpu.VMEM((PLANES, quarter, columns), jnp.float32)],
        compiler_params=limits,
    )(
        where,
        *received,
        q_gain.reshape(1, -1),
        kv_gain.reshape(1, -1),
        jnp.concatenate([cosine, cosine], axis=1),
        jnp.concatenate([-sine, sine], axis=1),
    )


def solution(mesh):
    placed = (P(("section", "fsdp"), "ep"), P(), P(), P(), P("fsdp", "ep"))
    return jax.shard_map(
        on_device,
        mesh=mesh,
        in_specs=placed,
        out_specs=(P(("section", "fsdp", "ep"), None), P(("section", "fsdp", "ep"), None)),
        check_vma=False,
    )
```

```python
import functools

import jax
import jax.numpy as jnp
import numpy as np
from jax import lax
from jax.experimental import pallas as pl
from jax.experimental.pallas import tpu as pltpu
from jax.sharding import PartitionSpec as P

QL = 1536
KVL = 512
ROPE = 64
LENGTH = 4096


epsilon = 1e-06
rope_base = 10000.0
PLANES = 4
PARTS = 3
NEAR_COST, LAST_COST = 1, 2
TURNS = 3, 2, 1, 0
LANES = 128
PACK = 16
VMEM_LIMIT = 20 * 1024 * 1024

vmem = pl.BlockSpec(memory_space=pltpu.VMEM)
smem = pl.BlockSpec(memory_space=pltpu.SMEM)
anywhere = pl.BlockSpec(memory_space=pl.ANY)


def square_sums(values):
    return jnp.sum(values * values, axis=1, keepdims=True)


def product(gained, weight):
    return lax.dot_general(
        gained, weight, (((1,), (1,)), ((), ())), preferred_element_type=jnp.float32
    )


def near_kernel(layout, where, *refs):
    refs = list(refs)
    block_refs = [refs.pop(0) for _ in range(3)]
    gain_ref = refs.pop(0)
    source_refs = [[refs.pop(0) for _ in range(parts)] for parts in layout]
    total, squares, last_weight, blocks, weights, block_arrived, weight_arrived = refs
    width = blocks.shape[2]

    def weight_copy(entry, act):
        into = weights.at[entry]
        for source, parts in enumerate(source_refs):

            @pl.when(where[1, entry] == source)
            def _():
                at = pl.multiple_of(where[2, entry] * width, width)
                for part, ref in enumerate(parts):
                    height = ref.shape[0]
                    copy = pltpu.make_async_copy(
                        ref.at[:, pl.ds(at, width)],
                        into.at[pl.ds(part * height, height)],
                        weight_arrived.at[entry, part],
                    )
                    getattr(copy, act)()

    def block_copy(entry, act):
        copy = pltpu.make_async_copy(block_refs[entry], blocks.at[entry], block_arrived.at[entry])
        getattr(copy, act)()

    for entry in range(3):
        block_copy(entry, "start")
        weight_copy(entry, "start")
    weight_copy(3, "start")
    for entry in range(3):
        block_copy(entry, "wait")
        values = blocks[entry].astype(jnp.float32)
        at = pl.multiple_of(where[0, entry] * width, width)
        gained = (values * gain_ref[:, pl.ds(at, width)]).astype(jnp.bfloat16)
        weight_copy(entry, "wait")
        if entry == 0:
            squares[...] = square_sums(values)
            total[...] = product(gained, weights[entry])
        else:
            squares[...] += square_sums(values)
            total[...] += product(gained, weights[entry])
    weight_copy(3, "wait")
    at = pl.multiple_of(where[0, 3] * width, width)
    gained = weights[3].astype(jnp.float32) * gain_ref[:, pl.ds(at, width)]
    last_weight[...] = gained.astype(jnp.bfloat16)


def pack(rows, out_ref):
    count, columns = rows.shape
    main = columns // LANES * LANES
    for tile in range(main // LANES):
        tile_rows = rows[:, tile * LANES : (tile + 1) * LANES]
        out_ref[tile * count : (tile + 1) * count, :] = tile_rows.astype(jnp.bfloat16)
    rest = [rows[at : at + PACK, main:] for at in range(0, count, PACK)]
    spare = LANES - len(rest) * (columns - main)
    rest = jnp.concatenate(rest + [jnp.zeros((PACK, spare), jnp.float32)], axis=1)
    out_ref[main // LANES * count :, :] = rest.astype(jnp.bfloat16)


def unpack(packed_ref, into):
    count, columns = into.shape
    main = columns // LANES * LANES
    for tile in range(main // LANES):
        tile_rows = packed_ref[tile * count : (tile + 1) * count, :]
        into[:, tile * LANES : (tile + 1) * LANES] = tile_rows.astype(jnp.float32)
    rest = packed_ref[main // LANES * count :, :].astype(jnp.float32)
    width = columns - main
    into[:, main:] = jnp.concatenate(
        [rest[:, at * width : (at + 1) * width] for at in range(count // PACK)], axis=0
    )


def last_kernel(depth, quarter, where, *refs):
    refs = list(refs)
    block_ref, weight_ref, total_ref, squares_ref = [refs.pop(0) for _ in range(4)]
    scaled = refs.pop(-1)
    block = block_ref[...]
    squares = squares_ref[...] + square_sums(block.astype(jnp.float32))
    total = total_ref[...] + product(block, weight_ref[...])
    scaled[...] = total * lax.rsqrt(squares / depth + epsilon)
    for turn, out_ref in zip(TURNS, refs):
        at = pl.multiple_of(where[3, turn] * quarter, quarter)
        pack(scaled[pl.ds(at, quarter), :], out_ref)


def finish_kernel(where, *refs):
    refs = list(refs)
    part_refs = [refs.pop(0) for _ in range(len(refs) - 7)]
    q_gain_ref, kv_gain_ref, cosine_ref, sine_ref, query_ref, cache_ref, parts = refs
    for turn, ref in zip(TURNS, part_refs):
        unpack(ref, parts.at[where[3, turn]])
    latent = jnp.concatenate([parts[plane] for plane in range(PLANES)], axis=1)

    def normed(values, gain):
        mean_square = jnp.mean(values * values, axis=-1, keepdims=True)
        return (values * lax.rsqrt(mean_square + epsilon) * gain).astype(jnp.bfloat16)

    query_ref[...] = normed(latent[:, :QL], q_gain_ref[...])
    cache_ref[:, :KVL] = normed(latent[:, QL : QL + KVL], kv_gain_ref[...])
    half = ROPE // 2
    key = latent[:, QL + KVL :]
    turned = jnp.concatenate([key[:, half:], key[:, :half]], axis=1)
    cache_ref[:, KVL:] = (key * cosine_ref[...] + turned * sine_ref[...]).astype(jnp.bfloat16)


def tables(fsdp, shared):
    made = np.zeros((2, fsdp, PLANES, 4, PLANES), np.int32)
    per = PLANES // fsdp if shared else PLANES
    for core, y, z in np.ndindex(2, fsdp, PLANES):
        for column, block in enumerate((z, PLANES - 1 - z, z ^ 1, z ^ 2)):
            source, inside = 0, block % per
            if shared and block // per != y:
                source, inside = (1 if inside == core else 2), 0
            made[core, y, z, :3, column] = [block, source, inside]
        made[core, y, z, 3] = [z ^ turn for turn in range(PLANES)]
    return made


def on_device(hidden, attn_gain, q_gain, kv_gain, down_weight):
    row_count, width = hidden.shape
    section, fsdp = lax.axis_size("section"), lax.axis_size("fsdp")
    ep_index, fsdp_index = lax.axis_index("ep"), lax.axis_index("fsdp")
    assert lax.axis_size("ep") == PLANES
    quarter = row_count // PLANES
    weight = down_weight.T
    columns = weight.shape[0]
    shared = fsdp == 2 and section % 2 == 0
    place = (lax.axis_index("section") % 2, fsdp_index, ep_index, 0, 0)
    where = lax.dynamic_slice(tables(fsdp, shared), place, (1, 1, 1, 4, PLANES)).reshape(4, PLANES)
    gain = attn_gain.reshape(1, -1)

    mirrored = lax.ppermute(hidden, "ep", [(z, PLANES - 1 - z) for z in range(PLANES)])
    paired = lax.ppermute(hidden, "ep", [(z, z ^ 1) for z in range(PLANES)])
    if shared:
        core = lax.axis_index("section") % 2
        height = columns // PARTS
        here = [
            lax.dynamic_slice(weight, (part * height, core * width), (height, width))
            for part in range(PARTS)
        ]
        here = [lax.ppermute(part, "fsdp", [(0, 1), (1, 0)]) for part in here]
        cores = [(s, s ^ 1) for s in range(section)]
        sources = [[weight], here, [lax.ppermute(part, "section", cores) for part in here]]
    else:
        sources = [[lax.all_gather(weight, "fsdp", axis=1, tiled=True)]]
    far = lax.ppermute(mirrored, "ep", [(z, z ^ 1) for z in range(PLANES)])

    limits = pltpu.CompilerParams(vmem_limit_bytes=VMEM_LIMIT)

    def cost(microseconds):
        return pl.CostEstimate(
            flops=int(microseconds * 1.15e9), bytes_accessed=2 * row_count * width, transcendentals=0
        )

    total, squares, last_weight = pl.pallas_call(
        functools.partial(near_kernel, [len(parts) for parts in sources]),
        out_shape=(
            jax.ShapeDtypeStruct((row_count, columns), jnp.float32),
            jax.ShapeDtypeStruct((row_count, 1), jnp.float32),
            jax.ShapeDtypeStruct((columns, width), jnp.bfloat16),
        ),
        in_specs=[smem] + [anywhere] * 3 + [vmem] + [anywhere] * sum(len(parts) for parts in sources),
        out_specs=(vmem, vmem, vmem),
        scratch_shapes=[
            pltpu.VMEM((3, row_count, width), jnp.bfloat16),
            pltpu.VMEM((4, columns, width), jnp.bfloat16),
            pltpu.SemaphoreType.DMA((3,)),
            pltpu.SemaphoreType.DMA((4, PARTS)),
        ],
        compiler_params=limits,
        cost_estimate=cost(NEAR_COST),
    )(where, hidden, mirrored, paired, gain, *[part for parts in sources for part in parts])

    packed = columns // LANES * quarter + PACK
    messages = pl.pallas_call(
        functools.partial(last_kernel, PLANES * width, quarter),
        out_shape=(jax.ShapeDtypeStruct((packed, LANES), jnp.bfloat16),) * PLANES,
        in_specs=[smem] + [vmem] * 4,
        out_specs=(vmem,) * PLANES,
        scratch_shapes=[pltpu.VMEM((row_count, columns), jnp.float32)],
        compiler_params=limits,
        cost_estimate=cost(LAST_COST),
    )(where, far, last_weight, total, squares)
    received = []
    for turn, message in zip(TURNS, messages):
        moves = [
            (s * PLANES + z, (s + 1) % section * PLANES + (z ^ turn))
            for s in range(section)
            for z in range(PLANES)
        ]
        received.append(lax.ppermute(message, ("section", "ep"), moves))

    half = ROPE // 2
    position = (fsdp_index * row_count + ep_index * quarter + jnp.arange(quarter)) % LENGTH
    frequency = rope_base ** (-(jnp.arange(half).astype(jnp.float32) / half))
    angle = position.astype(jnp.float32)[:, None] * frequency[None, :]
    cosine, sine = jnp.cos(angle), jnp.sin(angle)
    return pl.pallas_call(
        finish_kernel,
        out_shape=(
            jax.ShapeDtypeStruct((quarter, QL), jnp.bfloat16),
            jax.ShapeDtypeStruct((quarter, KVL + ROPE), jnp.bfloat16),
        ),
        in_specs=[smem] + [vmem] * (len(received) + 4),
        out_specs=(vmem, vmem),
        scratch_shapes=[pltpu.VMEM((PLANES, quarter, columns), jnp.float32)],
        compiler_params=limits,
    )(
        where,
        *received,
        q_gain.reshape(1, -1),
        kv_gain.reshape(1, -1),
        jnp.concatenate([cosine, cosine], axis=1),
        jnp.concatenate([-sine, sine], axis=1),
    )


def solution(mesh):
    placed = (P(("section", "fsdp"), "ep"), P(), P(), P(), P("fsdp", "ep"))
    return jax.shard_map(
        on_device,
        mesh=mesh,
        in_specs=placed,
        out_specs=(P(("section", "fsdp", "ep"), None), P(("section", "fsdp", "ep"), None)),
        check_vma=False,
    )
```

```python
import functools

import jax
import jax.numpy as jnp
import numpy as np
from jax import lax
from jax.experimental import pallas as pl
from jax.experimental.pallas import tpu as pltpu
from jax.sharding import PartitionSpec as P

QL = 1536
KVL = 512
ROPE = 64
LENGTH = 4096


epsilon = 1e-06
rope_base = 10000.0
PLANES = 4
PARTS = 3
NEAR_COST, LAST_COST = 1, 2
TURNS = 3, 2, 1, 0
LANES = 128
PACK = 16
VMEM_LIMIT = 20 * 1024 * 1024

vmem = pl.BlockSpec(memory_space=pltpu.VMEM)
smem = pl.BlockSpec(memory_space=pltpu.SMEM)
anywhere = pl.BlockSpec(memory_space=pl.ANY)


def square_sums(values):
    return jnp.sum(values * values, axis=1, keepdims=True)


def product(gained, weight):
    return lax.dot_general(
        gained, weight, (((1,), (1,)), ((), ())), preferred_element_type=jnp.float32
    )


def near_kernel(layout, where, *refs):
    refs = list(refs)
    block_refs = [refs.pop(0) for _ in range(3)]
    gain_ref = refs.pop(0)
    source_refs = [[refs.pop(0) for _ in range(parts)] for parts in layout]
    total, squares, last_weight, blocks, weights, block_arrived, weight_arrived = refs
    width = blocks.shape[2]

    def weight_copy(entry, act):
        into = weights.at[entry]
        for source, parts in enumerate(source_refs):

            @pl.when(where[1, entry] == source)
            def _():
                at = pl.multiple_of(where[2, entry] * width, width)
                for part, ref in enumerate(parts):
                    height = ref.shape[0]
                    copy = pltpu.make_async_copy(
                        ref.at[:, pl.ds(at, width)],
                        into.at[pl.ds(part * height, height)],
                        weight_arrived.at[entry, part],
                    )
                    getattr(copy, act)()

    def block_copy(entry, act):
        copy = pltpu.make_async_copy(block_refs[entry], blocks.at[entry], block_arrived.at[entry])
        getattr(copy, act)()

    for entry in range(3):
        block_copy(entry, "start")
        weight_copy(entry, "start")
    weight_copy(3, "start")
    for entry in range(3):
        block_copy(entry, "wait")
        values = blocks[entry].astype(jnp.float32)
        at = pl.multiple_of(where[0, entry] * width, width)
        gained = (values * gain_ref[:, pl.ds(at, width)]).astype(jnp.bfloat16)
        weight_copy(entry, "wait")
        if entry == 0:
            squares[...] = square_sums(values)
            total[...] = product(gained, weights[entry])
        else:
            squares[...] += square_sums(values)
            total[...] += product(gained, weights[entry])
    weight_copy(3, "wait")
    at = pl.multiple_of(where[0, 3] * width, width)
    gained = weights[3].astype(jnp.float32) * gain_ref[:, pl.ds(at, width)]
    last_weight[...] = gained.astype(jnp.bfloat16)


def pack(rows, out_ref):
    count, columns = rows.shape
    main = columns // LANES * LANES
    for tile in range(main // LANES):
        tile_rows = rows[:, tile * LANES : (tile + 1) * LANES]
        out_ref[tile * count : (tile + 1) * count, :] = tile_rows.astype(jnp.bfloat16)
    rest = [rows[at : at + PACK, main:] for at in range(0, count, PACK)]
    spare = LANES - len(rest) * (columns - main)
    rest = jnp.concatenate(rest + [jnp.zeros((PACK, spare), jnp.float32)], axis=1)
    out_ref[main // LANES * count :, :] = rest.astype(jnp.bfloat16)


def unpack(packed_ref, into):
    count, columns = into.shape
    main = columns // LANES * LANES
    for tile in range(main // LANES):
        tile_rows = packed_ref[tile * count : (tile + 1) * count, :]
        into[:, tile * LANES : (tile + 1) * LANES] = tile_rows.astype(jnp.float32)
    rest = packed_ref[main // LANES * count :, :].astype(jnp.float32)
    width = columns - main
    into[:, main:] = jnp.concatenate(
        [rest[:, at * width : (at + 1) * width] for at in range(count // PACK)], axis=0
    )


def last_kernel(depth, quarter, where, *refs):
    refs = list(refs)
    block_ref, weight_ref, total_ref, squares_ref = [refs.pop(0) for _ in range(4)]
    scaled = refs.pop(-1)
    block = block_ref[...]
    squares = squares_ref[...] + square_sums(block.astype(jnp.float32))
    total = total_ref[...] + product(block, weight_ref[...])
    scaled[...] = total * lax.rsqrt(squares / depth + epsilon)
    for turn, out_ref in zip(TURNS, refs):
        at = pl.multiple_of(where[3, turn] * quarter, quarter)
        pack(scaled[pl.ds(at, quarter), :], out_ref)


def finish_kernel(where, *refs):
    refs = list(refs)
    part_refs = [refs.pop(0) for _ in range(len(refs) - 7)]
    q_gain_ref, kv_gain_ref, cosine_ref, sine_ref, query_ref, cache_ref, parts = refs
    for turn, ref in zip(TURNS, part_refs):
        unpack(ref, parts.at[where[3, turn]])
    latent = jnp.concatenate([parts[plane] for plane in range(PLANES)], axis=1)

    def normed(values, gain):
        mean_square = jnp.mean(values * values, axis=-1, keepdims=True)
        return (values * lax.rsqrt(mean_square + epsilon) * gain).astype(jnp.bfloat16)

    query_ref[...] = normed(latent[:, :QL], q_gain_ref[...])
    cache_ref[:, :KVL] = normed(latent[:, QL : QL + KVL], kv_gain_ref[...])
    half = ROPE // 2
    key = latent[:, QL + KVL :]
    turned = jnp.concatenate([key[:, half:], key[:, :half]], axis=1)
    cache_ref[:, KVL:] = (key * cosine_ref[...] + turned * sine_ref[...]).astype(jnp.bfloat16)


def tables(fsdp, shared):
    made = np.zeros((2, fsdp, PLANES, 4, PLANES), np.int32)
    per = PLANES // fsdp if shared else PLANES
    for core, y, z in np.ndindex(2, fsdp, PLANES):
        for column, block in enumerate((z, PLANES - 1 - z, z ^ 1, z ^ 2)):
            source, inside = 0, block % per
            if shared and block // per != y:
                source, inside = (1 if inside == core else 2), 0
            made[core, y, z, :3, column] = [block, source, inside]
        made[core, y, z, 3] = [z ^ turn for turn in range(PLANES)]
    return made


def on_device(hidden, attn_gain, q_gain, kv_gain, down_weight):
    row_count, width = hidden.shape
    section, fsdp = lax.axis_size("section"), lax.axis_size("fsdp")
    ep_index, fsdp_index = lax.axis_index("ep"), lax.axis_index("fsdp")
    assert lax.axis_size("ep") == PLANES
    quarter = row_count // PLANES
    weight = down_weight.T
    columns = weight.shape[0]
    shared = fsdp == 2 and section % 2 == 0
    place = (lax.axis_index("section") % 2, fsdp_index, ep_index, 0, 0)
    where = lax.dynamic_slice(tables(fsdp, shared), place, (1, 1, 1, 4, PLANES)).reshape(4, PLANES)
    gain = attn_gain.reshape(1, -1)

    def onward(target_of):
        moves = [
            (s * PLANES + z, (s + 1) % section * PLANES + target_of(z))
            for s in range(section)
            for z in range(PLANES)
        ]
        return lax.ppermute(hidden, ("section", "ep"), moves)

    mirrored = onward(lambda z: PLANES - 1 - z)
    paired = onward(lambda z: z ^ 1)
    own = onward(lambda z: z)
    if shared:
        core = lax.axis_index("section") % 2
        height = columns // PARTS
        here = [
            lax.dynamic_slice(weight, (part * height, core * width), (height, width))
            for part in range(PARTS)
        ]
        here = [lax.ppermute(part, "fsdp", [(0, 1), (1, 0)]) for part in here]
        cores = [(s, s ^ 1) for s in range(section)]
        sources = [[weight], here, [lax.ppermute(part, "section", cores) for part in here]]
    else:
        sources = [[lax.all_gather(weight, "fsdp", axis=1, tiled=True)]]
    far = lax.ppermute(mirrored, "ep", [(z, z ^ 1) for z in range(PLANES)])

    limits = pltpu.CompilerParams(vmem_limit_bytes=VMEM_LIMIT)

    def cost(microseconds):
        return pl.CostEstimate(
            flops=int(microseconds * 1.15e9), bytes_accessed=2 * row_count * width, transcendentals=0
        )

    total, squares, last_weight = pl.pallas_call(
        functools.partial(near_kernel, [len(parts) for parts in sources]),
        out_shape=(
            jax.ShapeDtypeStruct((row_count, columns), jnp.float32),
            jax.ShapeDtypeStruct((row_count, 1), jnp.float32),
            jax.ShapeDtypeStruct((columns, width), jnp.bfloat16),
        ),
        in_specs=[smem] + [anywhere] * 3 + [vmem] + [anywhere] * sum(len(parts) for parts in sources),
        out_specs=(vmem, vmem, vmem),
        scratch_shapes=[
            pltpu.VMEM((3, row_count, width), jnp.bfloat16),
            pltpu.VMEM((4, columns, width), jnp.bfloat16),
            pltpu.SemaphoreType.DMA((3,)),
            pltpu.SemaphoreType.DMA((4, PARTS)),
        ],
        compiler_params=limits,
        cost_estimate=cost(NEAR_COST),
    )(where, own, mirrored, paired, gain, *[part for parts in sources for part in parts])

    packed = columns // LANES * quarter + PACK
    messages = pl.pallas_call(
        functools.partial(last_kernel, PLANES * width, quarter),
        out_shape=(jax.ShapeDtypeStruct((packed, LANES), jnp.bfloat16),) * PLANES,
        in_specs=[smem] + [vmem] * 4,
        out_specs=(vmem,) * PLANES,
        scratch_shapes=[pltpu.VMEM((row_count, columns), jnp.float32)],
        compiler_params=limits,
        cost_estimate=cost(LAST_COST),
    )(where, far, last_weight, total, squares)
    received = []
    for turn, message in zip(TURNS, messages):
        if turn:
            message = lax.ppermute(message, "ep", [(z, z ^ turn) for z in range(PLANES)])
        received.append(message)

    half = ROPE // 2
    position = (fsdp_index * row_count + ep_index * quarter + jnp.arange(quarter)) % LENGTH
    frequency = rope_base ** (-(jnp.arange(half).astype(jnp.float32) / half))
    angle = position.astype(jnp.float32)[:, None] * frequency[None, :]
    cosine, sine = jnp.cos(angle), jnp.sin(angle)
    return pl.pallas_call(
        finish_kernel,
        out_shape=(
            jax.ShapeDtypeStruct((quarter, QL), jnp.bfloat16),
            jax.ShapeDtypeStruct((quarter, KVL + ROPE), jnp.bfloat16),
        ),
        in_specs=[smem] + [vmem] * (len(received) + 4),
        out_specs=(vmem, vmem),
        scratch_shapes=[pltpu.VMEM((PLANES, quarter, columns), jnp.float32)],
        compiler_params=limits,
    )(
        where,
        *received,
        q_gain.reshape(1, -1),
        kv_gain.reshape(1, -1),
        jnp.concatenate([cosine, cosine], axis=1),
        jnp.concatenate([-sine, sine], axis=1),
    )


def solution(mesh):
    placed = (P(("section", "fsdp"), "ep"), P(), P(), P(), P("fsdp", "ep"))
    return jax.shard_map(
        on_device,
        mesh=mesh,
        in_specs=placed,
        out_specs=(P(("section", "fsdp", "ep"), None), P(("section", "fsdp", "ep"), None)),
        check_vma=False,
    )
```

```python
import functools

import jax
import jax.numpy as jnp
import numpy as np
from jax import lax
from jax.experimental import pallas as pl
from jax.experimental.pallas import tpu as pltpu
from jax.sharding import PartitionSpec as P

QL = 1536
KVL = 512
ROPE = 64
LENGTH = 4096


epsilon = 1e-06
rope_base = 10000.0
PLANES = 4
PARTS = 3
NEAR_COST, LAST_COST = 1, 2
TURNS = 3, 2, 1, 0
LANES = 128
PACK = 16
VMEM_LIMIT = 20 * 1024 * 1024

vmem = pl.BlockSpec(memory_space=pltpu.VMEM)
smem = pl.BlockSpec(memory_space=pltpu.SMEM)
anywhere = pl.BlockSpec(memory_space=pl.ANY)


def square_sums(values):
    return jnp.sum(values * values, axis=1, keepdims=True)


def product(gained, weight):
    return lax.dot_general(
        gained, weight, (((1,), (1,)), ((), ())), preferred_element_type=jnp.float32
    )


def near_kernel(layout, where, *refs):
    refs = list(refs)
    block_refs = [refs.pop(0) for _ in range(3)]
    gain_ref = refs.pop(0)
    source_refs = [[refs.pop(0) for _ in range(parts)] for parts in layout]
    total, squares, last_weight, blocks, weights, block_arrived, weight_arrived = refs
    width = blocks.shape[2]

    def weight_copy(entry, act):
        into = weights.at[entry]
        for source, parts in enumerate(source_refs):

            @pl.when(where[1, entry] == source)
            def _():
                at = pl.multiple_of(where[2, entry] * width, width)
                for part, ref in enumerate(parts):
                    height = ref.shape[0]
                    copy = pltpu.make_async_copy(
                        ref.at[:, pl.ds(at, width)],
                        into.at[pl.ds(part * height, height)],
                        weight_arrived.at[entry, part],
                    )
                    getattr(copy, act)()

    def block_copy(entry, act):
        copy = pltpu.make_async_copy(block_refs[entry], blocks.at[entry], block_arrived.at[entry])
        getattr(copy, act)()

    for entry in range(3):
        block_copy(entry, "start")
        weight_copy(entry, "start")
    weight_copy(3, "start")
    for entry in range(3):
        block_copy(entry, "wait")
        values = blocks[entry].astype(jnp.float32)
        at = pl.multiple_of(where[0, entry] * width, width)
        gained = (values * gain_ref[:, pl.ds(at, width)]).astype(jnp.bfloat16)
        weight_copy(entry, "wait")
        if entry == 0:
            squares[...] = square_sums(values)
            total[...] = product(gained, weights[entry])
        else:
            squares[...] += square_sums(values)
            total[...] += product(gained, weights[entry])
    weight_copy(3, "wait")
    at = pl.multiple_of(where[0, 3] * width, width)
    gained = weights[3].astype(jnp.float32) * gain_ref[:, pl.ds(at, width)]
    last_weight[...] = gained.astype(jnp.bfloat16)


def pack(rows, out_ref):
    count, columns = rows.shape
    main = columns // LANES * LANES
    for tile in range(main // LANES):
        tile_rows = rows[:, tile * LANES : (tile + 1) * LANES]
        out_ref[tile * count : (tile + 1) * count, :] = tile_rows.astype(jnp.bfloat16)
    rest = [rows[at : at + PACK, main:] for at in range(0, count, PACK)]
    spare = LANES - len(rest) * (columns - main)
    rest = jnp.concatenate(rest + [jnp.zeros((PACK, spare), jnp.float32)], axis=1)
    out_ref[main // LANES * count :, :] = rest.astype(jnp.bfloat16)


def unpack(packed_ref, into):
    count, columns = into.shape
    main = columns // LANES * LANES
    for tile in range(main // LANES):
        tile_rows = packed_ref[tile * count : (tile + 1) * count, :]
        into[:, tile * LANES : (tile + 1) * LANES] = tile_rows.astype(jnp.float32)
    rest = packed_ref[main // LANES * count :, :].astype(jnp.float32)
    width = columns - main
    into[:, main:] = jnp.concatenate(
        [rest[:, at * width : (at + 1) * width] for at in range(count // PACK)], axis=0
    )


def last_kernel(depth, quarter, where, *refs):
    refs = list(refs)
    block_ref, weight_ref, total_ref, squares_ref = [refs.pop(0) for _ in range(4)]
    scaled = refs.pop(-1)
    block = block_ref[...]
    squares = squares_ref[...] + square_sums(block.astype(jnp.float32))
    total = total_ref[...] + product(block, weight_ref[...])
    scaled[...] = total * lax.rsqrt(squares / depth + epsilon)
    for turn, out_ref in zip(TURNS, refs):
        at = pl.multiple_of(where[3, turn] * quarter, quarter)
        pack(scaled[pl.ds(at, quarter), :], out_ref)


def finish_kernel(where, *refs):
    refs = list(refs)
    part_refs = [refs.pop(0) for _ in range(len(refs) - 7)]
    q_gain_ref, kv_gain_ref, cosine_ref, sine_ref, query_ref, cache_ref, parts = refs
    for turn, ref in zip(TURNS, part_refs):
        unpack(ref, parts.at[where[3, turn]])
    latent = jnp.concatenate([parts[plane] for plane in range(PLANES)], axis=1)

    def normed(values, gain):
        mean_square = jnp.mean(values * values, axis=-1, keepdims=True)
        return (values * lax.rsqrt(mean_square + epsilon) * gain).astype(jnp.bfloat16)

    query_ref[...] = normed(latent[:, :QL], q_gain_ref[...])
    cache_ref[:, :KVL] = normed(latent[:, QL : QL + KVL], kv_gain_ref[...])
    half = ROPE // 2
    key = latent[:, QL + KVL :]
    turned = jnp.concatenate([key[:, half:], key[:, :half]], axis=1)
    cache_ref[:, KVL:] = (key * cosine_ref[...] + turned * sine_ref[...]).astype(jnp.bfloat16)


def tables(fsdp, shared):
    made = np.zeros((2, fsdp, PLANES, 4, PLANES), np.int32)
    per = PLANES // fsdp if shared else PLANES
    for core, y, z in np.ndindex(2, fsdp, PLANES):
        for column, block in enumerate((z, PLANES - 1 - z, z ^ 1, z ^ 2)):
            source, inside = 0, block % per
            if shared and block // per != y:
                source, inside = (1 if inside == core else 2), 0
            made[core, y, z, :3, column] = [block, source, inside]
        made[core, y, z, 3] = [z ^ turn for turn in range(PLANES)]
    return made


def on_device(hidden, attn_gain, q_gain, kv_gain, down_weight):
    row_count, width = hidden.shape
    section, fsdp = lax.axis_size("section"), lax.axis_size("fsdp")
    ep_index, fsdp_index = lax.axis_index("ep"), lax.axis_index("fsdp")
    assert lax.axis_size("ep") == PLANES
    quarter = row_count // PLANES
    weight = down_weight.T
    columns = weight.shape[0]
    shared = fsdp == 2 and section % 2 == 0
    place = (lax.axis_index("section") % 2, fsdp_index, ep_index, 0, 0)
    where = lax.dynamic_slice(tables(fsdp, shared), place, (1, 1, 1, 4, PLANES)).reshape(4, PLANES)
    gain = attn_gain.reshape(1, -1)

    def onward(block, target_of):
        moves = [
            (s * PLANES + z, (s + 1) % section * PLANES + target_of(z))
            for s in range(section)
            for z in range(PLANES)
        ]
        return lax.ppermute(block, ("section", "ep"), moves)

    mirrored = onward(hidden, lambda z: PLANES - 1 - z)
    paired = onward(hidden, lambda z: z ^ 1)
    late = hidden
    if shared:
        core = lax.axis_index("section") % 2
        height = columns // PARTS
        here = [
            lax.dynamic_slice(weight, (part * height, core * width), (height, width))
            for part in range(PARTS)
        ]
        here = [lax.ppermute(part, "fsdp", [(0, 1), (1, 0)]) for part in here]
        late, here[0] = lax.optimization_barrier((hidden, here[0]))
        cores = [(s, s ^ 1) for s in range(section)]
        sources = [[weight], here, [lax.ppermute(part, "section", cores) for part in here]]
    else:
        sources = [[lax.all_gather(weight, "fsdp", axis=1, tiled=True)]]
    own = onward(late, lambda z: z)
    far = lax.ppermute(mirrored, "ep", [(z, z ^ 1) for z in range(PLANES)])

    limits = pltpu.CompilerParams(vmem_limit_bytes=VMEM_LIMIT)

    def cost(microseconds):
        return pl.CostEstimate(
            flops=int(microseconds * 1.15e9), bytes_accessed=2 * row_count * width, transcendentals=0
        )

    total, squares, last_weight = pl.pallas_call(
        functools.partial(near_kernel, [len(parts) for parts in sources]),
        out_shape=(
            jax.ShapeDtypeStruct((row_count, columns), jnp.float32),
            jax.ShapeDtypeStruct((row_count, 1), jnp.float32),
            jax.ShapeDtypeStruct((columns, width), jnp.bfloat16),
        ),
        in_specs=[smem] + [anywhere] * 3 + [vmem] + [anywhere] * sum(len(parts) for parts in sources),
        out_specs=(vmem, vmem, vmem),
        scratch_shapes=[
            pltpu.VMEM((3, row_count, width), jnp.bfloat16),
            pltpu.VMEM((4, columns, width), jnp.bfloat16),
            pltpu.SemaphoreType.DMA((3,)),
            pltpu.SemaphoreType.DMA((4, PARTS)),
        ],
        compiler_params=limits,
        cost_estimate=cost(NEAR_COST),
    )(where, own, mirrored, paired, gain, *[part for parts in sources for part in parts])

    packed = columns // LANES * quarter + PACK
    messages = pl.pallas_call(
        functools.partial(last_kernel, PLANES * width, quarter),
        out_shape=(jax.ShapeDtypeStruct((packed, LANES), jnp.bfloat16),) * PLANES,
        in_specs=[smem] + [vmem] * 4,
        out_specs=(vmem,) * PLANES,
        scratch_shapes=[pltpu.VMEM((row_count, columns), jnp.float32)],
        compiler_params=limits,
        cost_estimate=cost(LAST_COST),
    )(where, far, last_weight, total, squares)
    received = []
    for turn, message in zip(TURNS, messages):
        if turn:
            message = lax.ppermute(message, "ep", [(z, z ^ turn) for z in range(PLANES)])
        received.append(message)

    half = ROPE // 2
    position = (fsdp_index * row_count + ep_index * quarter + jnp.arange(quarter)) % LENGTH
    frequency = rope_base ** (-(jnp.arange(half).astype(jnp.float32) / half))
    angle = position.astype(jnp.float32)[:, None] * frequency[None, :]
    cosine, sine = jnp.cos(angle), jnp.sin(angle)
    return pl.pallas_call(
        finish_kernel,
        out_shape=(
            jax.ShapeDtypeStruct((quarter, QL), jnp.bfloat16),
            jax.ShapeDtypeStruct((quarter, KVL + ROPE), jnp.bfloat16),
        ),
        in_specs=[smem] + [vmem] * (len(received) + 4),
        out_specs=(vmem, vmem),
        scratch_shapes=[pltpu.VMEM((PLANES, quarter, columns), jnp.float32)],
        compiler_params=limits,
    )(
        where,
        *received,
        q_gain.reshape(1, -1),
        kv_gain.reshape(1, -1),
        jnp.concatenate([cosine, cosine], axis=1),
        jnp.concatenate([-sine, sine], axis=1),
    )


def solution(mesh):
    placed = (P(("section", "fsdp"), "ep"), P(), P(), P(), P("fsdp", "ep"))
    return jax.shard_map(
        on_device,
        mesh=mesh,
        in_specs=placed,
        out_specs=(P(("section", "fsdp", "ep"), None), P(("section", "fsdp", "ep"), None)),
        check_vma=False,
    )
```

```python
import functools

import jax
import jax.numpy as jnp
import numpy as np
from jax import lax
from jax.experimental import pallas as pl
from jax.experimental.pallas import tpu as pltpu
from jax.sharding import PartitionSpec as P

QL = 1536
KVL = 512
ROPE = 64
LENGTH = 4096


epsilon = 1e-06
rope_base = 10000.0
PLANES = 4
PARTS = 3
NEAR_COST, LAST_COST = 1, 2
TURNS = 3, 2, 1, 0
LANES = 128
PACK = 16
VMEM_LIMIT = 20 * 1024 * 1024

vmem = pl.BlockSpec(memory_space=pltpu.VMEM)
smem = pl.BlockSpec(memory_space=pltpu.SMEM)
anywhere = pl.BlockSpec(memory_space=pl.ANY)


def square_sums(values):
    return jnp.sum(values * values, axis=1, keepdims=True)


def product(gained, weight):
    return lax.dot_general(
        gained, weight, (((1,), (1,)), ((), ())), preferred_element_type=jnp.float32
    )


def near_kernel(layout, where, *refs):
    refs = list(refs)
    block_refs = [refs.pop(0) for _ in range(3)]
    gain_ref = refs.pop(0)
    source_refs = [[refs.pop(0) for _ in range(parts)] for parts in layout]
    total, squares, last_weight, blocks, weights, block_arrived, weight_arrived = refs
    width = blocks.shape[2]

    def weight_copy(entry, act):
        into = weights.at[entry]
        for source, parts in enumerate(source_refs):

            @pl.when(where[1, entry] == source)
            def _():
                at = pl.multiple_of(where[2, entry] * width, width)
                for part, ref in enumerate(parts):
                    height = ref.shape[0]
                    copy = pltpu.make_async_copy(
                        ref.at[:, pl.ds(at, width)],
                        into.at[pl.ds(part * height, height)],
                        weight_arrived.at[entry, part],
                    )
                    getattr(copy, act)()

    def block_copy(entry, act):
        copy = pltpu.make_async_copy(block_refs[entry], blocks.at[entry], block_arrived.at[entry])
        getattr(copy, act)()

    for entry in range(3):
        block_copy(entry, "start")
        weight_copy(entry, "start")
    weight_copy(3, "start")
    for entry in range(3):
        block_copy(entry, "wait")
        values = blocks[entry].astype(jnp.float32)
        at = pl.multiple_of(where[0, entry] * width, width)
        gained = (values * gain_ref[:, pl.ds(at, width)]).astype(jnp.bfloat16)
        weight_copy(entry, "wait")
        if entry == 0:
            squares[...] = square_sums(values)
            total[...] = product(gained, weights[entry])
        else:
            squares[...] += square_sums(values)
            total[...] += product(gained, weights[entry])
    weight_copy(3, "wait")
    at = pl.multiple_of(where[0, 3] * width, width)
    gained = weights[3].astype(jnp.float32) * gain_ref[:, pl.ds(at, width)]
    last_weight[...] = gained.astype(jnp.bfloat16)


def pack(rows, out_ref):
    count, columns = rows.shape
    main = columns // LANES * LANES
    for tile in range(main // LANES):
        tile_rows = rows[:, tile * LANES : (tile + 1) * LANES]
        out_ref[tile * count : (tile + 1) * count, :] = tile_rows.astype(jnp.bfloat16)
    rest = [rows[at : at + PACK, main:] for at in range(0, count, PACK)]
    spare = LANES - len(rest) * (columns - main)
    rest = jnp.concatenate(rest + [jnp.zeros((PACK, spare), jnp.float32)], axis=1)
    out_ref[main // LANES * count :, :] = rest.astype(jnp.bfloat16)


def unpack(packed_ref, into):
    count, columns = into.shape
    main = columns // LANES * LANES
    for tile in range(main // LANES):
        tile_rows = packed_ref[tile * count : (tile + 1) * count, :]
        into[:, tile * LANES : (tile + 1) * LANES] = tile_rows.astype(jnp.float32)
    rest = packed_ref[main // LANES * count :, :].astype(jnp.float32)
    width = columns - main
    into[:, main:] = jnp.concatenate(
        [rest[:, at * width : (at + 1) * width] for at in range(count // PACK)], axis=0
    )


def last_kernel(depth, quarter, where, *refs):
    refs = list(refs)
    block_ref, weight_ref, total_ref, squares_ref = [refs.pop(0) for _ in range(4)]
    scaled = refs.pop(-1)
    block = block_ref[...]
    squares = squares_ref[...] + square_sums(block.astype(jnp.float32))
    total = total_ref[...] + product(block, weight_ref[...])
    scaled[...] = total * lax.rsqrt(squares / depth + epsilon)
    for turn, out_ref in zip(TURNS, refs):
        at = pl.multiple_of(where[3, turn] * quarter, quarter)
        if turn:
            pack(scaled[pl.ds(at, quarter), :], out_ref)
        else:
            out_ref[...] = scaled[pl.ds(at, quarter), :]


def finish_kernel(where, *refs):
    refs = list(refs)
    part_refs = [refs.pop(0) for _ in range(len(refs) - 7)]
    q_gain_ref, kv_gain_ref, cosine_ref, sine_ref, query_ref, cache_ref, parts = refs
    for turn, ref in zip(TURNS, part_refs):
        if turn:
            unpack(ref, parts.at[where[3, turn]])
        else:
            parts[where[3, turn]] = ref[...]
    latent = jnp.concatenate([parts[plane] for plane in range(PLANES)], axis=1)

    def normed(values, gain):
        mean_square = jnp.mean(values * values, axis=-1, keepdims=True)
        return (values * lax.rsqrt(mean_square + epsilon) * gain).astype(jnp.bfloat16)

    query_ref[...] = normed(latent[:, :QL], q_gain_ref[...])
    cache_ref[:, :KVL] = normed(latent[:, QL : QL + KVL], kv_gain_ref[...])
    half = ROPE // 2
    key = latent[:, QL + KVL :]
    turned = jnp.concatenate([key[:, half:], key[:, :half]], axis=1)
    cache_ref[:, KVL:] = (key * cosine_ref[...] + turned * sine_ref[...]).astype(jnp.bfloat16)


def tables(fsdp, shared):
    made = np.zeros((2, fsdp, PLANES, 4, PLANES), np.int32)
    per = PLANES // fsdp if shared else PLANES
    for core, y, z in np.ndindex(2, fsdp, PLANES):
        for column, block in enumerate((z, PLANES - 1 - z, z ^ 1, z ^ 2)):
            source, inside = 0, block % per
            if shared and block // per != y:
                source, inside = (1 if inside == core else 2), 0
            made[core, y, z, :3, column] = [block, source, inside]
        made[core, y, z, 3] = [z ^ turn for turn in range(PLANES)]
    return made


def on_device(hidden, attn_gain, q_gain, kv_gain, down_weight):
    row_count, width = hidden.shape
    section, fsdp = lax.axis_size("section"), lax.axis_size("fsdp")
    ep_index, fsdp_index = lax.axis_index("ep"), lax.axis_index("fsdp")
    assert lax.axis_size("ep") == PLANES
    quarter = row_count // PLANES
    weight = down_weight.T
    columns = weight.shape[0]
    shared = fsdp == 2 and section % 2 == 0
    place = (lax.axis_index("section") % 2, fsdp_index, ep_index, 0, 0)
    where = lax.dynamic_slice(tables(fsdp, shared), place, (1, 1, 1, 4, PLANES)).reshape(4, PLANES)
    gain = attn_gain.reshape(1, -1)

    def onward(block, target_of):
        moves = [
            (s * PLANES + z, (s + 1) % section * PLANES + target_of(z))
            for s in range(section)
            for z in range(PLANES)
        ]
        return lax.ppermute(block, ("section", "ep"), moves)

    mirrored = onward(hidden, lambda z: PLANES - 1 - z)
    paired = onward(hidden, lambda z: z ^ 1)
    late = hidden
    if shared:
        core = lax.axis_index("section") % 2
        height = columns // PARTS
        here = [
            lax.dynamic_slice(weight, (part * height, core * width), (height, width))
            for part in range(PARTS)
        ]
        here = [lax.ppermute(part, "fsdp", [(0, 1), (1, 0)]) for part in here]
        late, here[0] = lax.optimization_barrier((hidden, here[0]))
        cores = [(s, s ^ 1) for s in range(section)]
        sources = [[weight], here, [lax.ppermute(part, "section", cores) for part in here]]
    else:
        sources = [[lax.all_gather(weight, "fsdp", axis=1, tiled=True)]]
    own = onward(late, lambda z: z)
    far = lax.ppermute(mirrored, "ep", [(z, z ^ 1) for z in range(PLANES)])

    limits = pltpu.CompilerParams(vmem_limit_bytes=VMEM_LIMIT)

    def cost(microseconds):
        return pl.CostEstimate(
            flops=int(microseconds * 1.15e9), bytes_accessed=2 * row_count * width, transcendentals=0
        )

    total, squares, last_weight = pl.pallas_call(
        functools.partial(near_kernel, [len(parts) for parts in sources]),
        out_shape=(
            jax.ShapeDtypeStruct((row_count, columns), jnp.float32),
            jax.ShapeDtypeStruct((row_count, 1), jnp.float32),
            jax.ShapeDtypeStruct((columns, width), jnp.bfloat16),
        ),
        in_specs=[smem] + [anywhere] * 3 + [vmem] + [anywhere] * sum(len(parts) for parts in sources),
        out_specs=(vmem, vmem, vmem),
        scratch_shapes=[
            pltpu.VMEM((3, row_count, width), jnp.bfloat16),
            pltpu.VMEM((4, columns, width), jnp.bfloat16),
            pltpu.SemaphoreType.DMA((3,)),
            pltpu.SemaphoreType.DMA((4, PARTS)),
        ],
        compiler_params=limits,
        cost_estimate=cost(NEAR_COST),
    )(where, own, mirrored, paired, gain, *[part for parts in sources for part in parts])

    packed = columns // LANES * quarter + PACK
    messages = pl.pallas_call(
        functools.partial(last_kernel, PLANES * width, quarter),
        out_shape=[
            jax.ShapeDtypeStruct((packed, LANES), jnp.bfloat16)
            if turn
            else jax.ShapeDtypeStruct((quarter, columns), jnp.float32)
            for turn in TURNS
        ],
        in_specs=[smem] + [vmem] * 4,
        out_specs=[vmem] * PLANES,
        scratch_shapes=[pltpu.VMEM((row_count, columns), jnp.float32)],
        compiler_params=limits,
        cost_estimate=cost(LAST_COST),
    )(where, far, last_weight, total, squares)
    received = []
    for turn, message in zip(TURNS, messages):
        if turn:
            message = lax.ppermute(message, "ep", [(z, z ^ turn) for z in range(PLANES)])
        received.append(message)

    half = ROPE // 2
    position = (fsdp_index * row_count + ep_index * quarter + jnp.arange(quarter)) % LENGTH
    frequency = rope_base ** (-(jnp.arange(half).astype(jnp.float32) / half))
    angle = position.astype(jnp.float32)[:, None] * frequency[None, :]
    cosine, sine = jnp.cos(angle), jnp.sin(angle)
    return pl.pallas_call(
        finish_kernel,
        out_shape=(
            jax.ShapeDtypeStruct((quarter, QL), jnp.bfloat16),
            jax.ShapeDtypeStruct((quarter, KVL + ROPE), jnp.bfloat16),
        ),
        in_specs=[smem] + [vmem] * (len(received) + 4),
        out_specs=(vmem, vmem),
        scratch_shapes=[pltpu.VMEM((PLANES, quarter, columns), jnp.float32)],
        compiler_params=limits,
    )(
        where,
        *received,
        q_gain.reshape(1, -1),
        kv_gain.reshape(1, -1),
        jnp.concatenate([cosine, cosine], axis=1),
        jnp.concatenate([-sine, sine], axis=1),
    )


def solution(mesh):
    placed = (P(("section", "fsdp"), "ep"), P(), P(), P(), P("fsdp", "ep"))
    return jax.shard_map(
        on_device,
        mesh=mesh,
        in_specs=placed,
        out_specs=(P(("section", "fsdp", "ep"), None), P(("section", "fsdp", "ep"), None)),
        check_vma=False,
    )
```

```python
import functools

import jax
import jax.numpy as jnp
import numpy as np
from jax import lax
from jax.experimental import pallas as pl
from jax.experimental.pallas import tpu as pltpu
from jax.sharding import PartitionSpec as P

QL = 1536
KVL = 512
ROPE = 64
LENGTH = 4096


epsilon = 1e-06
rope_base = 10000.0
PLANES = 4
PARTS = 3
NEAR_COST, LAST_COST = 1, 2
TURNS = 3, 2, 1, 0
LANES = 128
PACK = 16
VMEM_LIMIT = 40 * 1024 * 1024

vmem = pl.BlockSpec(memory_space=pltpu.VMEM)
smem = pl.BlockSpec(memory_space=pltpu.SMEM)
anywhere = pl.BlockSpec(memory_space=pl.ANY)


def square_sums(values):
    return jnp.sum(values * values, axis=1, keepdims=True)


def product(gained, weight):
    return lax.dot_general(
        gained, weight, (((1,), (1,)), ((), ())), preferred_element_type=jnp.float32
    )


def near_kernel(layout, where, *refs):
    refs = list(refs)
    block_refs = [refs.pop(0) for _ in range(3)]
    gain_ref = refs.pop(0)
    source_refs = [[refs.pop(0) for _ in range(parts)] for parts in layout]
    total, squares, last_weight, blocks, weights, block_arrived, weight_arrived = refs
    width = blocks.shape[2]

    def weight_copy(entry, act):
        into = weights.at[entry]
        for source, parts in enumerate(source_refs):

            @pl.when(where[1, entry] == source)
            def _():
                at = pl.multiple_of(where[2, entry] * width, width)
                for part, ref in enumerate(parts):
                    height = ref.shape[0]
                    copy = pltpu.make_async_copy(
                        ref.at[:, pl.ds(at, width)],
                        into.at[pl.ds(part * height, height)],
                        weight_arrived.at[entry, part],
                    )
                    getattr(copy, act)()

    def block_copy(entry, act):
        copy = pltpu.make_async_copy(block_refs[entry], blocks.at[entry], block_arrived.at[entry])
        getattr(copy, act)()

    for entry in range(3):
        block_copy(entry, "start")
        weight_copy(entry, "start")
    weight_copy(3, "start")
    for entry in range(3):
        block_copy(entry, "wait")
        values = blocks[entry].astype(jnp.float32)
        at = pl.multiple_of(where[0, entry] * width, width)
        gained = (values * gain_ref[:, pl.ds(at, width)]).astype(jnp.bfloat16)
        weight_copy(entry, "wait")
        if entry == 0:
            squares[...] = square_sums(values)
            total[...] = product(gained, weights[entry])
        else:
            squares[...] += square_sums(values)
            total[...] += product(gained, weights[entry])
    weight_copy(3, "wait")
    at = pl.multiple_of(where[0, 3] * width, width)
    gained = weights[3].astype(jnp.float32) * gain_ref[:, pl.ds(at, width)]
    last_weight[...] = gained.astype(jnp.bfloat16)


def pack(rows, out_ref):
    count, columns = rows.shape
    main = columns // LANES * LANES
    for tile in range(main // LANES):
        tile_rows = rows[:, tile * LANES : (tile + 1) * LANES]
        out_ref[tile * count : (tile + 1) * count, :] = tile_rows.astype(jnp.bfloat16)
    rest = [rows[at : at + PACK, main:] for at in range(0, count, PACK)]
    spare = LANES - len(rest) * (columns - main)
    rest = jnp.concatenate(rest + [jnp.zeros((PACK, spare), jnp.float32)], axis=1)
    out_ref[main // LANES * count :, :] = rest.astype(jnp.bfloat16)


def unpack(packed_ref, into):
    count, columns = into.shape
    main = columns // LANES * LANES
    for tile in range(main // LANES):
        tile_rows = packed_ref[tile * count : (tile + 1) * count, :]
        into[:, tile * LANES : (tile + 1) * LANES] = tile_rows.astype(jnp.float32)
    rest = packed_ref[main // LANES * count :, :].astype(jnp.float32)
    width = columns - main
    into[:, main:] = jnp.concatenate(
        [rest[:, at * width : (at + 1) * width] for at in range(count // PACK)], axis=0
    )


def last_kernel(depth, quarter, where, *refs):
    refs = list(refs)
    block_ref, weight_ref, total_ref, squares_ref = [refs.pop(0) for _ in range(4)]
    scaled = refs.pop(-1)
    block = block_ref[...]
    squares = squares_ref[...] + square_sums(block.astype(jnp.float32))
    total = total_ref[...] + product(block, weight_ref[...])
    scaled[...] = total * lax.rsqrt(squares / depth + epsilon)
    for turn, out_ref in zip(TURNS, refs):
        at = pl.multiple_of(where[3, turn] * quarter, quarter)
        if turn:
            pack(scaled[pl.ds(at, quarter), :], out_ref)
        else:
            out_ref[...] = scaled[pl.ds(at, quarter), :]


def finish_kernel(where, *refs):
    refs = list(refs)
    part_refs = [refs.pop(0) for _ in range(len(refs) - 7)]
    q_gain_ref, kv_gain_ref, cosine_ref, sine_ref, query_ref, cache_ref, parts = refs
    for turn, ref in zip(TURNS, part_refs):
        if turn:
            unpack(ref, parts.at[where[3, turn]])
        else:
            parts[where[3, turn]] = ref[...]
    latent = jnp.concatenate([parts[plane] for plane in range(PLANES)], axis=1)

    def normed(values, gain):
        mean_square = jnp.mean(values * values, axis=-1, keepdims=True)
        return (values * lax.rsqrt(mean_square + epsilon) * gain).astype(jnp.bfloat16)

    query_ref[...] = normed(latent[:, :QL], q_gain_ref[...])
    cache_ref[:, :KVL] = normed(latent[:, QL : QL + KVL], kv_gain_ref[...])
    half = ROPE // 2
    key = latent[:, QL + KVL :]
    turned = jnp.concatenate([key[:, half:], key[:, :half]], axis=1)
    cache_ref[:, KVL:] = (key * cosine_ref[...] + turned * sine_ref[...]).astype(jnp.bfloat16)


def tables(fsdp, shared):
    made = np.zeros((2, fsdp, PLANES, 4, PLANES), np.int32)
    per = PLANES // fsdp if shared else PLANES
    for core, y, z in np.ndindex(2, fsdp, PLANES):
        for column, block in enumerate((z, PLANES - 1 - z, z ^ 1, z ^ 2)):
            source, inside = 0, block % per
            if shared and block // per != y:
                source, inside = (1 if inside == core else 2), 0
            made[core, y, z, :3, column] = [block, source, inside]
        made[core, y, z, 3] = [z ^ turn for turn in range(PLANES)]
    return made


def on_device(hidden, attn_gain, q_gain, kv_gain, down_weight):
    row_count, width = hidden.shape
    section, fsdp = lax.axis_size("section"), lax.axis_size("fsdp")
    ep_index, fsdp_index = lax.axis_index("ep"), lax.axis_index("fsdp")
    assert lax.axis_size("ep") == PLANES
    quarter = row_count // PLANES
    weight = down_weight.T
    columns = weight.shape[0]
    shared = fsdp == 2 and section % 2 == 0
    place = (lax.axis_index("section") % 2, fsdp_index, ep_index, 0, 0)
    where = lax.dynamic_slice(tables(fsdp, shared), place, (1, 1, 1, 4, PLANES)).reshape(4, PLANES)
    gain = attn_gain.reshape(1, -1)

    def onward(block, target_of):
        moves = [
            (s * PLANES + z, (s + 1) % section * PLANES + target_of(z))
            for s in range(section)
            for z in range(PLANES)
        ]
        return lax.ppermute(block, ("section", "ep"), moves)

    mirrored = onward(hidden, lambda z: PLANES - 1 - z)
    paired = onward(hidden, lambda z: z ^ 1)
    late = hidden
    if shared:
        core = lax.axis_index("section") % 2
        height = columns // PARTS
        here = [
            lax.dynamic_slice(weight, (part * height, core * width), (height, width))
            for part in range(PARTS)
        ]
        here = [lax.ppermute(part, "fsdp", [(0, 1), (1, 0)]) for part in here]
        late, here[0] = lax.optimization_barrier((hidden, here[0]))
        cores = [(s, s ^ 1) for s in range(section)]
        sources = [[weight], here, [lax.ppermute(part, "section", cores) for part in here]]
    else:
        sources = [[lax.all_gather(weight, "fsdp", axis=1, tiled=True)]]
    own = onward(late, lambda z: z)
    far = lax.ppermute(mirrored, "ep", [(z, z ^ 1) for z in range(PLANES)])

    limits = pltpu.CompilerParams(vmem_limit_bytes=VMEM_LIMIT)

    def cost(microseconds):
        return pl.CostEstimate(
            flops=int(microseconds * 1.15e9), bytes_accessed=2 * row_count * width, transcendentals=0
        )

    total, squares, last_weight = pl.pallas_call(
        functools.partial(near_kernel, [len(parts) for parts in sources]),
        out_shape=(
            jax.ShapeDtypeStruct((row_count, columns), jnp.float32),
            jax.ShapeDtypeStruct((row_count, 1), jnp.float32),
            jax.ShapeDtypeStruct((columns, width), jnp.bfloat16),
        ),
        in_specs=[smem] + [anywhere] * 3 + [vmem] + [anywhere] * sum(len(parts) for parts in sources),
        out_specs=(vmem, vmem, vmem),
        scratch_shapes=[
            pltpu.VMEM((3, row_count, width), jnp.bfloat16),
            pltpu.VMEM((4, columns, width), jnp.bfloat16),
            pltpu.SemaphoreType.DMA((3,)),
            pltpu.SemaphoreType.DMA((4, PARTS)),
        ],
        compiler_params=limits,
        cost_estimate=cost(NEAR_COST),
    )(where, own, mirrored, paired, gain, *[part for parts in sources for part in parts])

    packed = columns // LANES * quarter + PACK
    messages = pl.pallas_call(
        functools.partial(last_kernel, PLANES * width, quarter),
        out_shape=[
            jax.ShapeDtypeStruct((packed, LANES), jnp.bfloat16)
            if turn
            else jax.ShapeDtypeStruct((quarter, columns), jnp.float32)
            for turn in TURNS
        ],
        in_specs=[smem] + [vmem] * 4,
        out_specs=[vmem] * PLANES,
        scratch_shapes=[pltpu.VMEM((row_count, columns), jnp.float32)],
        compiler_params=limits,
        cost_estimate=cost(LAST_COST),
    )(where, far, last_weight, total, squares)
    received = []
    for turn, message in zip(TURNS, messages):
        if turn:
            message = lax.ppermute(message, "ep", [(z, z ^ turn) for z in range(PLANES)])
        received.append(message)

    half = ROPE // 2
    position = (fsdp_index * row_count + ep_index * quarter + jnp.arange(quarter)) % LENGTH
    frequency = rope_base ** (-(jnp.arange(half).astype(jnp.float32) / half))
    angle = position.astype(jnp.float32)[:, None] * frequency[None, :]
    cosine, sine = jnp.cos(angle), jnp.sin(angle)
    return pl.pallas_call(
        finish_kernel,
        out_shape=(
            jax.ShapeDtypeStruct((quarter, QL), jnp.bfloat16),
            jax.ShapeDtypeStruct((quarter, KVL + ROPE), jnp.bfloat16),
        ),
        in_specs=[smem] + [vmem] * (len(received) + 4),
        out_specs=(vmem, vmem),
        scratch_shapes=[pltpu.VMEM((PLANES, quarter, columns), jnp.float32)],
        compiler_params=limits,
    )(
        where,
        *received,
        q_gain.reshape(1, -1),
        kv_gain.reshape(1, -1),
        jnp.concatenate([cosine, cosine], axis=1),
        jnp.concatenate([-sine, sine], axis=1),
    )


def solution(mesh):
    placed = (P(("section", "fsdp"), "ep"), P(), P(), P(), P("fsdp", "ep"))
    return jax.shard_map(
        on_device,
        mesh=mesh,
        in_specs=placed,
        out_specs=(P(("section", "fsdp", "ep"), None), P(("section", "fsdp", "ep"), None)),
        check_vma=False,
    )
```
